32 devices in a mesh: row: 8 (over z, x), col: 4 (over y, core).
Axes of the slice: x: 2, y: 2, z: 4, core: 2. Of those that a mesh axis runs over, the one named last changes fastest.
Arguments:
- deposit_maps: float32 [1024, 8192], P('row', 'col'), may hold values from -30 to 30, as said below
- test_matrix: float32 [8192, 256], P('col'), may hold values from -1 to 1
Outputs:
- scaled_basis: float32 [1024, 256], P('row')
- projected: float32 [256, 8192], P('row', 'col')
The draws below stay inside these ranges and needn't reach their ends.
Inputs may be any that keep to these rules, and one draw needn't show every extreme that they name: `deposit_maps`: a dense real matrix.
All inputs are finite; a program needn't handle non-finite values.
Results may differ from the reference program's by a relative error of at most 0.0003.
Values sent between devices are 32-bit elements; how exact they have to be, the bound alone decides.
A program may use at most 64 MiB of HBM per device.

```python
import math
import jax
import jax.numpy as jnp
from jax import lax

N = 8192
K = 256
ROWS = 1024


def draw_deposit_maps(key, part):
    subkeys = jax.random.split(jax.random.fold_in(key, 7), 7)
    ramp_values = jnp.arange(ROWS, dtype=jnp.float32) / (ROWS - 1)
    entries = jnp.clip(jax.random.normal(subkeys[0], (ROWS, N), jnp.float32), -5.0, 5.0)
    row_scale = 10.0 ** (0.5 * ramp_values + 0.5 * jax.random.uniform(subkeys[1], (ROWS,), jnp.float32))
    column_scale = 10.0 ** jax.random.uniform(subkeys[2], (N,), jnp.float32)
    floor_part = entries * column_scale[None, :]
    spread = jnp.sqrt(jnp.mean(floor_part * floor_part))
    rank_count = K // 2
    fraction = (1.0 - math.sqrt(K / N)) * (1.0 - math.sqrt(K / ROWS))
    top_amplitude = 300.0 * fraction / math.sqrt(K) * spread
    decay_steps = jnp.arange(rank_count, dtype=jnp.float32) / (rank_count - 1)
    amplitudes = top_amplitude * 10.0 ** (-2.5 * decay_steps)
    left_factor = jnp.clip(jax.random.normal(subkeys[5], (ROWS, rank_count), jnp.float32), -6.0, 6.0)
    right_factor = jnp.clip(jax.random.normal(subkeys[6], (rank_count, N), jnp.float32), -6.0, 6.0)
    structured = jnp.dot(left_factor * amplitudes[None, :], right_factor, preferred_element_type=jnp.float32, precision=lax.Precision.HIGHEST)
    normalizer = 1.0 / (top_amplitude * math.sqrt(ROWS))
    total = (floor_part + structured) * row_scale[:, None] * normalizer
    return jnp.clip(total, -30.0, 30.0)


def draw_test_matrix(key, part):
    subkey = jax.random.fold_in(key, 11)
    entries = jnp.clip(jax.random.normal(subkey, (N, K), jnp.float32), -5.0, 5.0)
    return entries / math.sqrt(N)


def setup_inputs(seed: int = 0) -> dict:
    seeds = jax.random.split(jax.random.key(seed), 3)
    deposit_maps = draw_deposit_maps(jax.random.fold_in(seeds[2], 71), 0)
    test_matrix = draw_test_matrix(jax.random.fold_in(seeds[2], 71), 0)
    return {"deposit_maps": deposit_maps, "test_matrix": test_matrix}


def apply_factor(current, gram_matrix):
    lower_factor = jnp.linalg.cholesky(gram_matrix)
    identity = jnp.eye(gram_matrix.shape[0], dtype=jnp.float32)
    inverse = jax.scipy.linalg.solve_triangular(lower_factor, identity, lower=True)
    return jnp.dot(current.astype(jnp.float32), inverse.T.astype(jnp.float32), preferred_element_type=jnp.float32, precision=lax.Precision.HIGHEST)

def reference(deposit_maps, test_matrix):
    sketch = jnp.dot(deposit_maps.astype(jnp.float32), test_matrix.astype(jnp.float32), preferred_element_type=jnp.float32, precision=lax.Precision.HIGHEST)
    current = sketch
    for sweep_index in range(2):
        gram_matrix = jnp.dot(current.T.astype(jnp.float32), current.astype(jnp.float32), preferred_element_type=jnp.float32, precision=lax.Precision.HIGHEST)
        current = apply_factor(current, gram_matrix)
    scaled_basis = current * math.sqrt(ROWS)
    projected = jnp.dot(current.T.astype(jnp.float32), deposit_maps.astype(jnp.float32), preferred_element_type=jnp.float32, precision=lax.Precision.HIGHEST)
    return (scaled_basis, projected)
```

```python
import functools
import math

import jax
import jax.numpy as jnp
from jax import lax
from jax.experimental import pallas as pl
from jax.experimental.pallas import tpu as pltpu
from jax.sharding import PartitionSpec as P

MESH = pl.DeviceIdType.MESH
VMEM = pl.BlockSpec(memory_space=pltpu.VMEM)
BLOCK = 32


def dot(left, right, contract):
    return lax.dot_general(
        left,
        right,
        ((contract[:1], contract[1:]), ((), ())),
        preferred_element_type=jnp.float32,
        precision=lax.Precision.HIGHEST,
    )


def small_inverse(block):
    b = block.shape[0]
    row_index = lax.broadcasted_iota(jnp.int32, (b, 128), 0)
    lane = lax.broadcasted_iota(jnp.int32, (b, 128), 1)
    work = jnp.where(lane < b, block, jnp.where(lane == row_index + b, 1.0, 0.0))
    scale = jnp.zeros((b, 128), jnp.float32)
    for k in range(b):
        column = jnp.broadcast_to(work[:, k : k + 1], (b, 128))
        row = jnp.broadcast_to(work[k : k + 1, :], (b, 128))
        pivot = jnp.broadcast_to(column[k : k + 1, :], (b, 128))
        scale = jnp.where(row_index == k, pivot, scale)
        work = jnp.where(row_index > k, work - (column / pivot) * row, work)
    work = work * lax.rsqrt(scale)
    return work[:, b : 2 * b]


def factor_inverse(x_ref):
    size = x_ref.shape[0]
    lane = lax.broadcasted_iota(jnp.int32, (BLOCK, size), 1)
    row_index = lax.broadcasted_iota(jnp.int32, (BLOCK, size), 0)
    all_rows = lax.broadcasted_iota(jnp.int32, (size, size), 0)
    all_lanes = lax.broadcasted_iota(jnp.int32, (size, size), 1)

    def step(i, carry):
        start = pl.multiple_of(i * BLOCK, BLOCK)
        rows = x_ref[pl.ds(start, BLOCK), :]
        diagonal = pltpu.roll(rows, lax.rem(size - start, size), 1)[:, :128]
        inverse = small_inverse(diagonal)
        inside = (lane >= start) & (lane < start + BLOCK)
        rows = jnp.where(inside, jnp.where(lane == start + row_index, 1.0, 0.0), rows)
        done = dot(inverse, rows, (1, 0))
        upper = jnp.where(lane >= start + BLOCK, done, 0.0)
        update = dot(upper, done, (0, 0))
        below = all_rows >= start + BLOCK
        cleared = (all_lanes >= start) & (all_lanes < start + BLOCK)
        x_ref[...] = jnp.where(below & cleared, 0.0, x_ref[...]) - update
        x_ref[pl.ds(start, BLOCK), :] = done
        return carry

    lax.fori_loop(0, size // BLOCK, step, 0)
    x_ref[...] = jnp.where(all_lanes <= all_rows, x_ref[...], 0.0)


def first_pass_kernel(
    dims, maps_ref, test_ref, basis_ref, gram_ref, proj_ref,
    part, landed, sketch, columns, factor,
    col_send, col_recv, z_send, z_recv, xy_send, xy_recv, core_send, core_recv, a_send, a_recv,
):
    n_row, n_col, n_z = dims
    r, c = lax.axis_index("row"), lax.axis_index("col")
    z, x = r // 2, lax.rem(r, 2)
    y, core = c // 2, lax.rem(c, 2)
    width = columns.shape[-1]
    size = factor.shape[0]

    def device(z_to, x_to, y_to, core_to):
        return (z_to * 2 + x_to, y_to * 2 + core_to)

    barrier = pltpu.get_barrier_semaphore()
    for k in range(1, n_row):
        pl.semaphore_signal(
            barrier, inc=1, device_id=(lax.rem(r + k, n_row), c), device_id_type=MESH
        )
    for k in range(1, n_col):
        pl.semaphore_signal(
            barrier, inc=1, device_id=(r, lax.rem(c + k, n_col)), device_id_type=MESH
        )

    sub = part.shape[1]
    depth = maps_ref.shape[-1]
    own_maps = maps_ref[...].reshape(n_col * sub, depth)
    part[...] = dot(own_maps, test_ref[...], (1, 0)).reshape(part.shape)
    pl.semaphore_wait(barrier, n_row - 1 + n_col - 1)

    def send(source, target, send_sem, recv_sem, to):
        copy = pltpu.make_async_remote_copy(
            src_ref=source, dst_ref=target, send_sem=send_sem, recv_sem=recv_sem,
            device_id=to, device_id_type=MESH,
        )
        copy.start()
        return copy

    copies = []
    for k in range(1, n_col):
        to = lax.rem(c + k, n_col)
        copies.append(
            send(part.at[to], landed.at[k - 1], col_send.at[k - 1], col_recv.at[k - 1], (r, to))
        )
    total = part[c]
    for k, copy in enumerate(copies):
        copy.wait_recv()
        total = total + landed[k]
    sketch[y, core, x, z] = total
    sent = list(copies)

    copies = []
    for k in range(1, n_z):
        mine = sketch.at[y, core, x, z]
        to = device(lax.rem(z + k, n_z), x, y, core)
        copies.append(send(mine, mine, z_send.at[k - 1], z_recv.at[k - 1], to))
    for copy in copies:
        copy.wait_recv()
    sent += copies

    x_peer, y_peer = device(z, 1 - x, y, core), device(z, x, 1 - y, core)
    half = n_z // 2
    low, high = pl.ds(0, half), pl.ds(half, half)
    a = sketch.at[y, core, x, low]
    b = sketch.at[y, core, x, high]
    copies = [
        send(a, a, xy_send.at[0], xy_recv.at[0], x_peer),
        send(b, b, xy_send.at[1], xy_recv.at[1], y_peer),
    ]
    for copy in copies:
        copy.wait_recv()
    sent += copies
    a = sketch.at[y, core, :, low]
    b = sketch.at[:, core, x, high]
    copies = [
        send(a, a, xy_send.at[2], xy_recv.at[2], y_peer),
        send(b, b, xy_send.at[3], xy_recv.at[3], x_peer),
    ]
    for copy in copies:
        copy.wait_recv()
    sent += copies

    mine = sketch.at[:, core]
    core_copy = send(mine, mine, core_send, core_recv, device(z, x, y, 1 - core))
    core_copy.wait_recv()
    sent.append(core_copy)

    a_copies = []
    for k in range(1, n_row):
        to = lax.rem(r + k, n_row)
        share = pl.ds(pl.multiple_of(to * width, width), width)
        a_copies.append(
            send(
                maps_ref.at[:, :, :, share], columns.at[:, :, x, z],
                a_send.at[k - 1], a_recv.at[k - 1], (to, c),
            )
        )
    share = pl.ds(pl.multiple_of(r * width, width), width)
    columns[:, :, x, z] = maps_ref[:, :, :, share]

    chunks = [(i, j) for i in range(n_col // 2) for j in range(2)]
    gram = None
    for i, j in chunks:
        rows = sketch[i, j].reshape(-1, size)
        term = dot(rows, rows, (0, 0))
        gram = term if gram is None else gram + term
    factor[...] = gram
    factor_inverse(factor)
    inverse = factor[...]
    for copy in sent:
        copy.wait_send()
    gram = None
    for i, j in chunks:
        rows = dot(sketch[i, j].reshape(-1, size), inverse, (1, 1))
        sketch[i, j] = rows.reshape(sketch.shape[2:])
        term = dot(rows, rows, (0, 0))
        gram = term if gram is None else gram + term
    gram_ref[...] = gram
    basis_ref[...] = sketch[:, :, x, z]
    for copy in a_copies:
        copy.wait()
    proj = None
    for i, j in chunks:
        term = dot(
            sketch[i, j].reshape(-1, size), columns[i, j].reshape(-1, width), (0, 0)
        )
        proj = term if proj is None else proj + term
    proj_ref[...] = proj


def second_pass_kernel(total_rows, gram_ref, basis_ref, proj_ref, scaled_ref, out_ref, factor):
    size = gram_ref.shape[0]
    row_index = lax.broadcasted_iota(jnp.int32, (size, size), 0)
    lane = lax.broadcasted_iota(jnp.int32, (size, size), 1)
    identity = jnp.where(row_index == lane, 1.0, 0.0)
    weight = jnp.where(lane < row_index, 1.0, 0.5 * identity)
    gram = gram_ref[...]
    error = gram - identity
    small = jnp.sum(error * error) <= 4e-4

    @pl.when(small)
    def _():
        inverse = identity - weight * error
        left = error - dot(weight * error, gram, (1, 0))
        residual = left - dot(identity + left, weight * error, (1, 1))
        factor[...] = inverse - dot(weight * residual, inverse, (1, 0))

    @pl.when(jnp.logical_not(small))
    def _():
        factor[...] = gram
        factor_inverse(factor)

    inverse = factor[...]
    scaled_ref[...] = dot(basis_ref[...], inverse, (1, 1)) * math.sqrt(total_rows)
    out_ref[...] = dot(inverse, proj_ref[...], (1, 0))


def spread_kernel(n_row, proj_ref, out_ref, send_sem, recv_sem):
    r, c = lax.axis_index("row"), lax.axis_index("col")
    width = proj_ref.shape[-1]
    barrier = pltpu.get_barrier_semaphore()
    for k in range(1, n_row):
        pl.semaphore_signal(
            barrier, inc=1, device_id=(lax.rem(r + k, n_row), c), device_id_type=MESH
        )
    share = pl.ds(pl.multiple_of(r * width, width), width)
    out_ref[:, share] = proj_ref[r]
    pl.semaphore_wait(barrier, n_row - 1)
    copies = []
    for k in range(1, n_row):
        to = lax.rem(r + k, n_row)
        copy = pltpu.make_async_remote_copy(
            src_ref=proj_ref.at[to], dst_ref=out_ref.at[:, share],
            send_sem=send_sem.at[k - 1], recv_sem=recv_sem.at[k - 1],
            device_id=(to, c), device_id_type=MESH,
        )
        copy.start()
        copies.append(copy)
    for copy in copies:
        copy.wait()


def gathered(deposit_maps, test_matrix):
    n_row, n_col = lax.axis_size("row"), lax.axis_size("col")
    rows, depth = deposit_maps.shape
    size = test_matrix.shape[1]
    sub, width, n_z = rows // n_col, depth // n_row, n_row // 2
    f32 = jnp.float32
    maps = deposit_maps.reshape(n_col // 2, 2, sub, depth)
    dma = pltpu.SemaphoreType.DMA
    basis, gram, proj = pl.pallas_call(
        functools.partial(first_pass_kernel, (n_row, n_col, n_z)),
        out_shape=(
            jax.ShapeDtypeStruct((n_col // 2, 2, sub, size), f32),
            jax.ShapeDtypeStruct((size, size), f32),
            jax.ShapeDtypeStruct((size, width), f32),
        ),
        in_specs=[VMEM, VMEM],
        out_specs=(VMEM, VMEM, VMEM),
        scratch_shapes=[
            pltpu.VMEM((n_col, sub, size), f32),
            pltpu.VMEM((n_col - 1, sub, size), f32),
            pltpu.VMEM((n_col // 2, 2, 2, n_z, sub, size), f32),
            pltpu.VMEM((n_col // 2, 2, 2, n_z, sub, width), f32),
            pltpu.VMEM((size, size), f32),
            dma((n_col - 1,)), dma((n_col - 1,)),
            dma((n_z - 1,)), dma((n_z - 1,)),
            dma((4,)), dma((4,)),
            dma, dma,
            dma((n_row - 1,)), dma((n_row - 1,)),
        ],
        compiler_params=pltpu.CompilerParams(
            collective_id=0, has_side_effects=True, vmem_limit_bytes=40 * 2**20
        ),
    )(maps, test_matrix)
    scaled, full = pl.pallas_call(
        functools.partial(second_pass_kernel, rows * n_row),
        out_shape=(
            jax.ShapeDtypeStruct((rows, size), f32),
            jax.ShapeDtypeStruct((size, width), f32),
        ),
        in_specs=[VMEM, VMEM, VMEM],
        out_specs=(VMEM, VMEM),
        scratch_shapes=[pltpu.VMEM((size, size), f32)],
        compiler_params=pltpu.CompilerParams(vmem_limit_bytes=32 * 2**20),
    )(gram, basis.reshape(rows, size), proj)
    projected = pl.pallas_call(
        functools.partial(spread_kernel, n_row),
        out_shape=jax.ShapeDtypeStruct((size // n_row, depth), f32),
        in_specs=[VMEM],
        out_specs=VMEM,
        scratch_shapes=[dma((n_row - 1,)), dma((n_row - 1,))],
        compiler_params=pltpu.CompilerParams(
            collective_id=1, has_side_effects=True, vmem_limit_bytes=32 * 2**20
        ),
    )(full.reshape(n_row, size // n_row, width))
    return scaled, projected


def apply_factor(current, gram_matrix):
    lower_factor = jnp.linalg.cholesky(gram_matrix)
    identity = jnp.eye(gram_matrix.shape[0], dtype=jnp.float32)
    inverse = jax.scipy.linalg.solve_triangular(lower_factor, identity, lower=True)
    return dot(current, inverse, (1, 1))


def summed(deposit_maps, test_matrix):
    current = lax.psum(dot(deposit_maps, test_matrix, (1, 0)), "col")
    for _ in range(2):
        gram_matrix = lax.psum(dot(current, current, (0, 0)), "row")
        current = apply_factor(current, gram_matrix)
    total_rows = current.shape[0] * lax.axis_size("row")
    projected = lax.psum_scatter(
        dot(current, deposit_maps, (0, 0)), "row", scatter_dimension=0, tiled=True
    )
    return current * math.sqrt(total_rows), projected


def on_device(deposit_maps, test_matrix):
    n_row, n_col = lax.axis_size("row"), lax.axis_size("col")
    rows, depth = deposit_maps.shape
    size = test_matrix.shape[1]
    fits = (
        n_col == 4
        and n_row % 4 == 0
        and rows % (n_col * 16) == 0
        and depth % (n_row * 128) == 0
        and size % (n_row * 8) == 0
        and size % 128 == 0
        and rows * n_row * size * 4 <= 4 * 2**20
        and depth * rows * 4 <= 4 * 2**20
        and depth * size * 4 <= 4 * 2**20
    )
    if fits:
        return gathered(deposit_maps, test_matrix)
    return summed(deposit_maps, test_matrix)


def solution(mesh):
    placed = (P("row", "col"), P("col", None))
    return jax.shard_map(
        on_device,
        mesh=mesh,
        in_specs=placed,
        out_specs=(P("row", None), P("row", "col")),
        check_vma=False,
    )
```

```python
import functools
import math

import jax
import jax.numpy as jnp
from jax import lax
from jax.experimental import pallas as pl
from jax.experimental.pallas import tpu as pltpu
from jax.sharding import PartitionSpec as P

MESH = pl.DeviceIdType.MESH
VMEM = pl.BlockSpec(memory_space=pltpu.VMEM)
BLOCK = 64
PIECES = 4


def dot(left, right, contract):
    return lax.dot_general(
        left,
        right,
        ((contract[:1], contract[1:]), ((), ())),
        preferred_element_type=jnp.float32,
        precision=lax.Precision.HIGHEST,
    )


def small_inverse(block):
    b = block.shape[0]
    row_index = lax.broadcasted_iota(jnp.int32, (b, 128), 0)
    lane = lax.broadcasted_iota(jnp.int32, (b, 128), 1)
    work = jnp.where(lane < b, block, jnp.where(lane == row_index + b, 1.0, 0.0))
    tiles = [work[8 * t : 8 * t + 8, :] for t in range(b // 8)]
    row_index = lax.broadcasted_iota(jnp.int32, (8, 128), 0)
    finished = []
    for group in range(b // 8):
        head, below = tiles[0], tiles[1:]
        first = 8 * group
        wide = [
            [jnp.broadcast_to(tile[:, first + m : first + m + 1], (8, 128)) for m in range(8)]
            for tile in tiles
        ]
        entry = {
            (i, j): jnp.broadcast_to(wide[0][j][i : i + 1, :], (8, 128))
            for i in range(8)
            for j in range(i + 1)
        }
        rows = [jnp.broadcast_to(head[i : i + 1, :], (8, 128)) for i in range(8)]
        pivots = jnp.ones((8, 128), jnp.float32)
        for m in range(8):
            pivot = entry[m, m]
            over = 1.0 / pivot
            for i in range(m + 1, 8):
                factor = entry[i, m] * over
                for j in range(m + 1, i + 1):
                    entry[i, j] = entry[i, j] - factor * entry[j, m]
                rows[i] = rows[i] - factor * rows[m]
                for columns in wide[1:]:
                    columns[i] = columns[i] - factor * columns[m]
            for t in range(len(below)):
                below[t] = below[t] - (wide[t + 1][m] * over) * rows[m]
            pivots = jnp.where(row_index == m, pivot, pivots)
        merged = rows[0]
        for m in range(1, 8):
            merged = jnp.where(row_index == m, rows[m], merged)
        finished.append(merged * lax.rsqrt(pivots))
        tiles = below
    return jnp.concatenate(finished, axis=0)[:, b : 2 * b]


def factor_inverse(x_ref):
    size = x_ref.shape[0]
    lane = lax.broadcasted_iota(jnp.int32, (BLOCK, size), 1)
    row_index = lax.broadcasted_iota(jnp.int32, (BLOCK, size), 0)
    all_rows = lax.broadcasted_iota(jnp.int32, (size, size), 0)
    all_lanes = lax.broadcasted_iota(jnp.int32, (size, size), 1)

    def step(i, carry):
        start = pl.multiple_of(i * BLOCK, BLOCK)
        rows = x_ref[pl.ds(start, BLOCK), :]
        diagonal = pltpu.roll(rows, lax.rem(size - start, size), 1)[:, :128]
        inverse = small_inverse(diagonal)
        inside = (lane >= start) & (lane < start + BLOCK)
        rows = jnp.where(inside, jnp.where(lane == start + row_index, 1.0, 0.0), rows)
        done = dot(inverse, rows, (1, 0))
        upper = jnp.where(lane >= start + BLOCK, done, 0.0)
        update = dot(upper, done, (0, 0))
        below = all_rows >= start + BLOCK
        cleared = (all_lanes >= start) & (all_lanes < start + BLOCK)
        x_ref[...] = jnp.where(below & cleared, 0.0, x_ref[...]) - update
        x_ref[pl.ds(start, BLOCK), :] = done
        return carry

    lax.fori_loop(0, size // BLOCK, step, 0)
    x_ref[...] = jnp.where(all_lanes <= all_rows, x_ref[...], 0.0)


def first_pass_kernel(
    dims, maps_hbm, test_hbm, basis_ref, gram_ref, proj_ref,
    maps_ref, test_ref, load, part, landed, sketch, columns, factor,
    col_send, col_recv, z_send, z_recv, xy_send, xy_recv, core_send, core_recv, a_send, a_recv,
):
    n_row, n_col, n_z = dims
    r, c = lax.axis_index("row"), lax.axis_index("col")
    z, x = r // 2, lax.rem(r, 2)
    y, core = c // 2, lax.rem(c, 2)
    width = columns.shape[-1]
    size = factor.shape[0]

    def device(z_to, x_to, y_to, core_to):
        return (z_to * 2 + x_to, y_to * 2 + core_to)

    pieces = load.shape[0]
    depth = maps_ref.shape[-1]
    step = depth // pieces
    loads = []
    for k in range(pieces):
        span = pl.ds(k * step, step)
        loads.append((
            pltpu.make_async_copy(
                maps_hbm.at[:, :, :, span], maps_ref.at[:, :, :, span], load.at[k, 0]
            ),
            pltpu.make_async_copy(test_hbm.at[span], test_ref.at[span], load.at[k, 1]),
        ))
        for copy in loads[-1]:
            copy.start()

    barrier = pltpu.get_barrier_semaphore()
    for k in range(1, n_row):
        pl.semaphore_signal(
            barrier, inc=1, device_id=(lax.rem(r + k, n_row), c), device_id_type=MESH
        )
    for k in range(1, n_col):
        pl.semaphore_signal(
            barrier, inc=1, device_id=(r, lax.rem(c + k, n_col)), device_id_type=MESH
        )

    sub = part.shape[1]
    partial = None
    for k in range(pieces):
        for copy in loads[k]:
            copy.wait()
        span = pl.ds(k * step, step)
        term = dot(maps_ref[:, :, :, span].reshape(n_col * sub, step), test_ref[span], (1, 0))
        partial = term if partial is None else partial + term
    part[...] = partial.reshape(part.shape)
    pl.semaphore_wait(barrier, n_row - 1 + n_col - 1)

    def send(source, target, send_sem, recv_sem, to):
        copy = pltpu.make_async_remote_copy(
            src_ref=source, dst_ref=target, send_sem=send_sem, recv_sem=recv_sem,
            device_id=to, device_id_type=MESH,
        )
        copy.start()
        return copy

    copies = []
    for k in range(1, n_col):
        to = lax.rem(c + k, n_col)
        copies.append(
            send(part.at[to], landed.at[k - 1], col_send.at[k - 1], col_recv.at[k - 1], (r, to))
        )
    total = part[c]
    for k, copy in enumerate(copies):
        copy.wait_recv()
        total = total + landed[k]
    sketch[y, core, x, z] = total
    sent = list(copies)

    copies = []
    for k in range(1, n_z):
        mine = sketch.at[y, core, x, z]
        to = device(lax.rem(z + k, n_z), x, y, core)
        copies.append(send(mine, mine, z_send.at[k - 1], z_recv.at[k - 1], to))
    for copy in copies:
        copy.wait_recv()
    sent += copies

    x_peer, y_peer = device(z, 1 - x, y, core), device(z, x, 1 - y, core)
    half = n_z // 2
    low, high = pl.ds(0, half), pl.ds(half, half)
    a = sketch.at[y, core, x, low]
    b = sketch.at[y, core, x, high]
    copies = [
        send(a, a, xy_send.at[0], xy_recv.at[0], x_peer),
        send(b, b, xy_send.at[1], xy_recv.at[1], y_peer),
    ]
    for copy in copies:
        copy.wait_recv()
    sent += copies
    a = sketch.at[y, core, :, low]
    b = sketch.at[:, core, x, high]
    copies = [
        send(a, a, xy_send.at[2], xy_recv.at[2], y_peer),
        send(b, b, xy_send.at[3], xy_recv.at[3], x_peer),
    ]
    for copy in copies:
        copy.wait_recv()
    sent += copies

    mine = sketch.at[:, core]
    core_copy = send(mine, mine, core_send, core_recv, device(z, x, y, 1 - core))
    core_copy.wait_recv()
    sent.append(core_copy)

    a_copies = []
    for k in range(1, n_row):
        to = lax.rem(r + k, n_row)
        share = pl.ds(pl.multiple_of(to * width, width), width)
        a_copies.append(
            send(
                maps_ref.at[:, :, :, share], columns.at[:, :, x, z],
                a_send.at[k - 1], a_recv.at[k - 1], (to, c),
            )
        )
    share = pl.ds(pl.multiple_of(r * width, width), width)
    columns[:, :, x, z] = maps_ref[:, :, :, share]

    chunks = [(i, j) for i in range(n_col // 2) for j in range(2)]
    gram = None
    for i, j in chunks:
        rows = sketch[i, j].reshape(-1, size)
        term = dot(rows, rows, (0, 0))
        gram = term if gram is None else gram + term
    factor[...] = gram
    factor_inverse(factor)
    inverse = factor[...]
    for copy in sent:
        copy.wait_send()
    gram = None
    for i, j in chunks:
        rows = dot(sketch[i, j].reshape(-1, size), inverse, (1, 1))
        sketch[i, j] = rows.reshape(sketch.shape[2:])
        term = dot(rows, rows, (0, 0))
        gram = term if gram is None else gram + term
    gram_ref[...] = gram
    basis_ref[...] = sketch[:, :, x, z]
    for copy in a_copies:
        copy.wait()
    proj = None
    for i, j in chunks:
        term = dot(
            sketch[i, j].reshape(-1, size), columns[i, j].reshape(-1, width), (0, 0)
        )
        proj = term if proj is None else proj + term
    proj_ref[...] = proj


def second_pass_kernel(total_rows, gram_ref, basis_ref, proj_ref, scaled_ref, out_ref, factor):
    size = gram_ref.shape[0]
    row_index = lax.broadcasted_iota(jnp.int32, (size, size), 0)
    lane = lax.broadcasted_iota(jnp.int32, (size, size), 1)
    identity = jnp.where(row_index == lane, 1.0, 0.0)
    weight = jnp.where(lane < row_index, 1.0, 0.5 * identity)
    gram = gram_ref[...]
    error = gram - identity
    small = jnp.sum(error * error) <= 4e-4

    @pl.when(small)
    def _():
        inverse = identity - weight * error
        left = error - dot(weight * error, gram, (1, 0))
        residual = left - dot(identity + left, weight * error, (1, 1))
        factor[...] = inverse - dot(weight * residual, inverse, (1, 0))

    @pl.when(jnp.logical_not(small))
    def _():
        factor[...] = gram
        factor_inverse(factor)

    inverse = factor[...]
    scaled_ref[...] = dot(basis_ref[...], inverse, (1, 1)) * math.sqrt(total_rows)
    out_ref[...] = dot(inverse, proj_ref[...], (1, 0))


def spread_kernel(n_row, proj_ref, out_ref, send_sem, recv_sem):
    r, c = lax.axis_index("row"), lax.axis_index("col")
    width = proj_ref.shape[-1]
    barrier = pltpu.get_barrier_semaphore()
    for k in range(1, n_row):
        pl.semaphore_signal(
            barrier, inc=1, device_id=(lax.rem(r + k, n_row), c), device_id_type=MESH
        )
    share = pl.ds(pl.multiple_of(r * width, width), width)
    out_ref[:, share] = proj_ref[r]
    pl.semaphore_wait(barrier, n_row - 1)
    copies = []
    for k in range(1, n_row):
        to = lax.rem(r + k, n_row)
        copy = pltpu.make_async_remote_copy(
            src_ref=proj_ref.at[to], dst_ref=out_ref.at[:, share],
            send_sem=send_sem.at[k - 1], recv_sem=recv_sem.at[k - 1],
            device_id=(to, c), device_id_type=MESH,
        )
        copy.start()
        copies.append(copy)
    for copy in copies:
        copy.wait()


def gathered(deposit_maps, test_matrix):
    n_row, n_col = lax.axis_size("row"), lax.axis_size("col")
    rows, depth = deposit_maps.shape
    size = test_matrix.shape[1]
    sub, width, n_z = rows // n_col, depth // n_row, n_row // 2
    f32 = jnp.float32
    maps = deposit_maps.reshape(n_col // 2, 2, sub, depth)
    dma = pltpu.SemaphoreType.DMA
    basis, gram, proj = pl.pallas_call(
        functools.partial(first_pass_kernel, (n_row, n_col, n_z)),
        out_shape=(
            jax.ShapeDtypeStruct((n_col // 2, 2, sub, size), f32),
            jax.ShapeDtypeStruct((size, size), f32),
            jax.ShapeDtypeStruct((size, width), f32),
        ),
        in_specs=[pl.BlockSpec(memory_space=pl.ANY)] * 2,
        out_specs=(VMEM, VMEM, VMEM),
        scratch_shapes=[
            pltpu.VMEM(maps.shape, f32),
            pltpu.VMEM(test_matrix.shape, f32),
            dma((PIECES, 2)),
            pltpu.VMEM((n_col, sub, size), f32),
            pltpu.VMEM((n_col - 1, sub, size), f32),
            pltpu.VMEM((n_col // 2, 2, 2, n_z, sub, size), f32),
            pltpu.VMEM((n_col // 2, 2, 2, n_z, sub, width), f32),
            pltpu.VMEM((size, size), f32),
            dma((n_col - 1,)), dma((n_col - 1,)),
            dma((n_z - 1,)), dma((n_z - 1,)),
            dma((4,)), dma((4,)),
            dma, dma,
            dma((n_row - 1,)), dma((n_row - 1,)),
        ],
        compiler_params=pltpu.CompilerParams(
            collective_id=0, has_side_effects=True, vmem_limit_bytes=56 * 2**20
        ),
    )(maps, test_matrix)
    scaled, full = pl.pallas_call(
        functools.partial(second_pass_kernel, rows * n_row),
        out_shape=(
            jax.ShapeDtypeStruct((rows, size), f32),
            jax.ShapeDtypeStruct((size, width), f32),
        ),
        in_specs=[VMEM, VMEM, VMEM],
        out_specs=(VMEM, VMEM),
        scratch_shapes=[pltpu.VMEM((size, size), f32)],
        compiler_params=pltpu.CompilerParams(vmem_limit_bytes=32 * 2**20),
    )(gram, basis.reshape(rows, size), proj)
    projected = pl.pallas_call(
        functools.partial(spread_kernel, n_row),
        out_shape=jax.ShapeDtypeStruct((size // n_row, depth), f32),
        in_specs=[VMEM],
        out_specs=VMEM,
        scratch_shapes=[dma((n_row - 1,)), dma((n_row - 1,))],
        compiler_params=pltpu.CompilerParams(
            collective_id=1, has_side_effects=True, vmem_limit_bytes=32 * 2**20
        ),
    )(full.reshape(n_row, size // n_row, width))
    return scaled, projected


def apply_factor(current, gram_matrix):
    lower_factor = jnp.linalg.cholesky(gram_matrix)
    identity = jnp.eye(gram_matrix.shape[0], dtype=jnp.float32)
    inverse = jax.scipy.linalg.solve_triangular(lower_factor, identity, lower=True)
    return dot(current, inverse, (1, 1))


def summed(deposit_maps, test_matrix):
    current = lax.psum(dot(deposit_maps, test_matrix, (1, 0)), "col")
    for _ in range(2):
        gram_matrix = lax.psum(dot(current, current, (0, 0)), "row")
        current = apply_factor(current, gram_matrix)
    total_rows = current.shape[0] * lax.axis_size("row")
    projected = lax.psum_scatter(
        dot(current, deposit_maps, (0, 0)), "row", scatter_dimension=0, tiled=True
    )
    return current * math.sqrt(total_rows), projected


def on_device(deposit_maps, test_matrix):
    n_row, n_col = lax.axis_size("row"), lax.axis_size("col")
    rows, depth = deposit_maps.shape
    size = test_matrix.shape[1]
    fits = (
        n_col == 4
        and n_row % 4 == 0
        and rows % (n_col * 16) == 0
        and depth % (n_row * 128) == 0
        and size % (n_row * 8) == 0
        and size % 128 == 0
        and depth % (PIECES * 128) == 0
        and rows * n_row * size * 4 <= 4 * 2**20
        and depth * rows * 4 <= 4 * 2**20
        and depth * size * 4 <= 4 * 2**20
    )
    if fits:
        return gathered(deposit_maps, test_matrix)
    return summed(deposit_maps, test_matrix)


def solution(mesh):
    placed = (P("row", "col"), P("col", None))
    return jax.shard_map(
        on_device,
        mesh=mesh,
        in_specs=placed,
        out_specs=(P("row", None), P("row", "col")),
        check_vma=False,
    )
```

```python
import functools
import math

import jax
import jax.numpy as jnp
from jax import lax
from jax.experimental import pallas as pl
from jax.experimental.pallas import tpu as pltpu
from jax.sharding import PartitionSpec as P

MESH = pl.DeviceIdType.MESH
VMEM = pl.BlockSpec(memory_space=pltpu.VMEM)
BLOCK = 64
PIECES = 4
THREE = lax.Precision.HIGH


def dot(left, right, contract, precision=lax.Precision.HIGHEST):
    return lax.dot_general(
        left,
        right,
        ((contract[:1], contract[1:]), ((), ())),
        preferred_element_type=jnp.float32,
        precision=precision,
    )


def small_inverse(block):
    b = block.shape[0]
    row_index = lax.broadcasted_iota(jnp.int32, (b, 128), 0)
    lane = lax.broadcasted_iota(jnp.int32, (b, 128), 1)
    work = jnp.where(lane < b, block, jnp.where(lane == row_index + b, 1.0, 0.0))
    tiles = [work[8 * t : 8 * t + 8, :] for t in range(b // 8)]
    row_index = lax.broadcasted_iota(jnp.int32, (8, 128), 0)
    finished = []
    for group in range(b // 8):
        head, below = tiles[0], tiles[1:]
        first = 8 * group
        wide = [
            [jnp.broadcast_to(tile[:, first + m : first + m + 1], (8, 128)) for m in range(8)]
            for tile in tiles
        ]
        entry = {
            (i, j): jnp.broadcast_to(wide[0][j][i : i + 1, :], (8, 128))
            for i in range(8)
            for j in range(i + 1)
        }
        rows = [jnp.broadcast_to(head[i : i + 1, :], (8, 128)) for i in range(8)]
        pivots = jnp.ones((8, 128), jnp.float32)
        for m in range(8):
            pivot = entry[m, m]
            over = 1.0 / pivot
            for i in range(m + 1, 8):
                factor = entry[i, m] * over
                for j in range(m + 1, i + 1):
                    entry[i, j] = entry[i, j] - factor * entry[j, m]
                rows[i] = rows[i] - factor * rows[m]
                for columns in wide[1:]:
                    columns[i] = columns[i] - factor * columns[m]
            for t in range(len(below)):
                below[t] = below[t] - (wide[t + 1][m] * over) * rows[m]
            pivots = jnp.where(row_index == m, pivot, pivots)
        merged = rows[0]
        for m in range(1, 8):
            merged = jnp.where(row_index == m, rows[m], merged)
        finished.append(merged * lax.rsqrt(pivots))
        tiles = below
    return jnp.concatenate(finished, axis=0)[:, b : 2 * b]


def factor_inverse(x_ref):
    size = x_ref.shape[0]
    lane = lax.broadcasted_iota(jnp.int32, (BLOCK, size), 1)
    row_index = lax.broadcasted_iota(jnp.int32, (BLOCK, size), 0)
    all_rows = lax.broadcasted_iota(jnp.int32, (size, size), 0)
    all_lanes = lax.broadcasted_iota(jnp.int32, (size, size), 1)

    def step(i, carry):
        start = pl.multiple_of(i * BLOCK, BLOCK)
        rows = x_ref[pl.ds(start, BLOCK), :]
        diagonal = pltpu.roll(rows, lax.rem(size - start, size), 1)[:, :128]
        inverse = small_inverse(diagonal)
        inside = (lane >= start) & (lane < start + BLOCK)
        rows = jnp.where(inside, jnp.where(lane == start + row_index, 1.0, 0.0), rows)
        done = dot(inverse, rows, (1, 0))
        upper = jnp.where(lane >= start + BLOCK, done, 0.0)
        update = dot(upper, done, (0, 0))
        below = all_rows >= start + BLOCK
        cleared = (all_lanes >= start) & (all_lanes < start + BLOCK)
        x_ref[...] = jnp.where(below & cleared, 0.0, x_ref[...]) - update
        x_ref[pl.ds(start, BLOCK), :] = done
        return carry

    lax.fori_loop(0, size // BLOCK, step, 0)
    x_ref[...] = jnp.where(all_lanes <= all_rows, x_ref[...], 0.0)


def first_pass_kernel(
    dims, maps_hbm, test_hbm, basis_ref, gram_ref, proj_ref,
    maps_ref, test_ref, load, part, landed, sketch, columns, factor,
    col_send, col_recv, z_send, z_recv, xy_send, xy_recv, core_send, core_recv, a_send, a_recv,
):
    n_row, n_col, n_z = dims
    r, c = lax.axis_index("row"), lax.axis_index("col")
    z, x = r // 2, lax.rem(r, 2)
    y, core = c // 2, lax.rem(c, 2)
    width = columns.shape[-1]
    size = factor.shape[0]

    def device(z_to, x_to, y_to, core_to):
        return (z_to * 2 + x_to, y_to * 2 + core_to)

    pieces = load.shape[0]
    depth = maps_ref.shape[-1]
    step = depth // pieces
    loads = []
    for k in range(pieces):
        span = pl.ds(k * step, step)
        loads.append((
            pltpu.make_async_copy(
                maps_hbm.at[:, :, :, span], maps_ref.at[:, :, :, span], load.at[k, 0]
            ),
            pltpu.make_async_copy(test_hbm.at[span], test_ref.at[span], load.at[k, 1]),
        ))
        for copy in loads[-1]:
            copy.start()

    barrier = pltpu.get_barrier_semaphore()
    for k in range(1, n_row):
        pl.semaphore_signal(
            barrier, inc=1, device_id=(lax.rem(r + k, n_row), c), device_id_type=MESH
        )
    for k in range(1, n_col):
        pl.semaphore_signal(
            barrier, inc=1, device_id=(r, lax.rem(c + k, n_col)), device_id_type=MESH
        )

    def send(source, target, send_sem, recv_sem, to):
        copy = pltpu.make_async_remote_copy(
            src_ref=source, dst_ref=target, send_sem=send_sem, recv_sem=recv_sem,
            device_id=to, device_id_type=MESH,
        )
        copy.start()
        return copy

    a_copies = []

    def exchange(steps_z, step_x):
        for step_z in steps_z:
            z_to, x_to = lax.rem(z + step_z, n_z), (1 - x if step_x else x)
            to = z_to * 2 + x_to
            span = pl.ds(pl.multiple_of(to * width, width), width)
            k = step_z * 2 + step_x - 1
            a_copies.append(
                send(
                    maps_ref.at[:, :, :, span], columns.at[:, :, x, z],
                    a_send.at[k], a_recv.at[k], (to, c),
                )
            )

    sub = part.shape[1]
    partial = None
    for copy, _ in loads:
        copy.wait()
    for k in range(pieces):
        if k == pieces // 2:
            pl.semaphore_wait(barrier, n_row - 1 + n_col - 1)
            exchange([n_z // 2], 0)
        loads[k][1].wait()
        span = pl.ds(k * step, step)
        term = dot(maps_ref[:, :, :, span].reshape(n_col * sub, step), test_ref[span], (1, 0))
        partial = term if partial is None else partial + term
    part[...] = partial.reshape(part.shape)
    copies = []
    for k in range(1, n_col):
        to = lax.rem(c + k, n_col)
        copies.append(
            send(part.at[to], landed.at[k - 1], col_send.at[k - 1], col_recv.at[k - 1], (r, to))
        )
    total = part[c]
    for k, copy in enumerate(copies):
        copy.wait_recv()
        total = total + landed[k]
    sketch[y, core, x, z] = total
    sent = list(copies)

    copies = []
    for k in range(1, n_z):
        mine = sketch.at[y, core, x, z]
        to = device(lax.rem(z + k, n_z), x, y, core)
        copies.append(send(mine, mine, z_send.at[k - 1], z_recv.at[k - 1], to))
    for copy in copies:
        copy.wait_recv()
    sent += copies
    exchange([k for k in range(1, n_z) if k != n_z // 2], 0)

    x_peer, y_peer = device(z, 1 - x, y, core), device(z, x, 1 - y, core)
    half = n_z // 2
    low, high = pl.ds(0, half), pl.ds(half, half)
    a = sketch.at[y, core, x, low]
    b = sketch.at[y, core, x, high]
    copies = [
        send(a, a, xy_send.at[0], xy_recv.at[0], x_peer),
        send(b, b, xy_send.at[1], xy_recv.at[1], y_peer),
    ]
    for copy in copies:
        copy.wait_recv()
    sent += copies
    a = sketch.at[y, core, :, low]
    b = sketch.at[:, core, x, high]
    copies = [
        send(a, a, xy_send.at[2], xy_recv.at[2], y_peer),
        send(b, b, xy_send.at[3], xy_recv.at[3], x_peer),
    ]
    for copy in copies:
        copy.wait_recv()
    sent += copies

    mine = sketch.at[:, core]
    core_copy = send(mine, mine, core_send, core_recv, device(z, x, y, 1 - core))
    sent.append(core_copy)
    exchange(range(n_z), 1)
    share = pl.ds(pl.multiple_of(r * width, width), width)
    columns[:, :, x, z] = maps_ref[:, :, :, share]

    def half_gram(which):
        half_sum = None
        for i in range(n_col // 2):
            rows = sketch[i, which].reshape(-1, size)
            term = dot(rows, rows, (0, 0))
            half_sum = term if half_sum is None else half_sum + term
        return half_sum

    gram = half_gram(core)
    core_copy.wait_recv()
    gram = gram + half_gram(1 - core)
    chunks = [(i, j) for i in range(n_col // 2) for j in range(2)]
    factor[...] = gram
    factor_inverse(factor)
    inverse = factor[...]
    for copy in sent:
        copy.wait_send()
    gram = None
    for i, j in chunks:
        rows = dot(sketch[i, j].reshape(-1, size), inverse, (1, 1))
        sketch[i, j] = rows.reshape(sketch.shape[2:])
        term = dot(rows, rows, (0, 0), THREE)
        gram = term if gram is None else gram + term
    gram_ref[...] = gram
    basis_ref[...] = sketch[:, :, x, z]
    for copy in a_copies:
        copy.wait()
    proj = None
    for i, j in chunks:
        term = dot(
            sketch[i, j].reshape(-1, size), columns[i, j].reshape(-1, width), (0, 0),
            THREE,
        )
        proj = term if proj is None else proj + term
    proj_ref[...] = proj


def second_pass_kernel(total_rows, gram_ref, basis_ref, proj_ref, scaled_ref, out_ref, factor):
    size = gram_ref.shape[0]
    row_index = lax.broadcasted_iota(jnp.int32, (size, size), 0)
    lane = lax.broadcasted_iota(jnp.int32, (size, size), 1)
    identity = jnp.where(row_index == lane, 1.0, 0.0)
    weight = jnp.where(lane < row_index, 1.0, 0.5 * identity)
    gram = gram_ref[...]
    error = gram - identity
    small = jnp.sum(error * error) <= 4e-4

    @pl.when(small)
    def _():
        inverse = identity - weight * error
        left = error - dot(weight * error, gram, (1, 0))
        residual = left - dot(identity + left, weight * error, (1, 1))
        factor[...] = inverse - dot(weight * residual, inverse, (1, 0))

    @pl.when(jnp.logical_not(small))
    def _():
        factor[...] = gram
        factor_inverse(factor)

    inverse = factor[...]
    scaled_ref[...] = dot(basis_ref[...], inverse, (1, 1), THREE) * math.sqrt(total_rows)
    out_ref[...] = dot(inverse, proj_ref[...], (1, 0), THREE)


def spread_kernel(n_row, proj_ref, out_ref, send_sem, recv_sem):
    r, c = lax.axis_index("row"), lax.axis_index("col")
    width = proj_ref.shape[-1]
    barrier = pltpu.get_barrier_semaphore()
    for k in range(1, n_row):
        pl.semaphore_signal(
            barrier, inc=1, device_id=(lax.rem(r + k, n_row), c), device_id_type=MESH
        )
    share = pl.ds(pl.multiple_of(r * width, width), width)
    out_ref[:, share] = proj_ref[r]
    pl.semaphore_wait(barrier, n_row - 1)
    copies = []
    for k in range(1, n_row):
        to = lax.rem(r + k, n_row)
        copy = pltpu.make_async_remote_copy(
            src_ref=proj_ref.at[to], dst_ref=out_ref.at[:, share],
            send_sem=send_sem.at[k - 1], recv_sem=recv_sem.at[k - 1],
            device_id=(to, c), device_id_type=MESH,
        )
        copy.start()
        copies.append(copy)
    for copy in copies:
        copy.wait()


def gathered(deposit_maps, test_matrix):
    n_row, n_col = lax.axis_size("row"), lax.axis_size("col")
    rows, depth = deposit_maps.shape
    size = test_matrix.shape[1]
    sub, width, n_z = rows // n_col, depth // n_row, n_row // 2
    f32 = jnp.float32
    maps = deposit_maps.reshape(n_col // 2, 2, sub, depth)
    dma = pltpu.SemaphoreType.DMA
    basis, gram, proj = pl.pallas_call(
        functools.partial(first_pass_kernel, (n_row, n_col, n_z)),
        out_shape=(
            jax.ShapeDtypeStruct((n_col // 2, 2, sub, size), f32),
            jax.ShapeDtypeStruct((size, size), f32),
            jax.ShapeDtypeStruct((size, width), f32),
        ),
        in_specs=[pl.BlockSpec(memory_space=pltpu.HBM)] * 2,
        out_specs=(VMEM, VMEM, VMEM),
        scratch_shapes=[
            pltpu.VMEM(maps.shape, f32),
            pltpu.VMEM(test_matrix.shape, f32),
            dma((PIECES, 2)),
            pltpu.VMEM((n_col, sub, size), f32),
            pltpu.VMEM((n_col - 1, sub, size), f32),
            pltpu.VMEM((n_col // 2, 2, 2, n_z, sub, size), f32),
            pltpu.VMEM((n_col // 2, 2, 2, n_z, sub, width), f32),
            pltpu.VMEM((size, size), f32),
            dma((n_col - 1,)), dma((n_col - 1,)),
            dma((n_z - 1,)), dma((n_z - 1,)),
            dma((4,)), dma((4,)),
            dma, dma,
            dma((n_row - 1,)), dma((n_row - 1,)),
        ],
        compiler_params=pltpu.CompilerParams(
            collective_id=0, has_side_effects=True, vmem_limit_bytes=53 * 2**20
        ),
    )(maps, test_matrix)
    scaled, full = pl.pallas_call(
        functools.partial(second_pass_kernel, rows * n_row),
        out_shape=(
            jax.ShapeDtypeStruct((rows, size), f32),
            jax.ShapeDtypeStruct((size, width), f32),
        ),
        in_specs=[VMEM, VMEM, VMEM],
        out_specs=(VMEM, VMEM),
        scratch_shapes=[pltpu.VMEM((size, size), f32)],
        compiler_params=pltpu.CompilerParams(vmem_limit_bytes=32 * 2**20),
    )(gram, basis.reshape(rows, size), proj)
    projected = pl.pallas_call(
        functools.partial(spread_kernel, n_row),
        out_shape=jax.ShapeDtypeStruct((size // n_row, depth), f32),
        in_specs=[VMEM],
        out_specs=VMEM,
        scratch_shapes=[dma((n_row - 1,)), dma((n_row - 1,))],
        compiler_params=pltpu.CompilerParams(
            collective_id=1, has_side_effects=True, vmem_limit_bytes=32 * 2**20
        ),
    )(full.reshape(n_row, size // n_row, width))
    return scaled, projected


def apply_factor(current, gram_matrix):
    lower_factor = jnp.linalg.cholesky(gram_matrix)
    identity = jnp.eye(gram_matrix.shape[0], dtype=jnp.float32)
    inverse = jax.scipy.linalg.solve_triangular(lower_factor, identity, lower=True)
    return dot(current, inverse, (1, 1))


def summed(deposit_maps, test_matrix):
    current = lax.psum(dot(deposit_maps, test_matrix, (1, 0)), "col")
    for _ in range(2):
        gram_matrix = lax.psum(dot(current, current, (0, 0)), "row")
        current = apply_factor(current, gram_matrix)
    total_rows = current.shape[0] * lax.axis_size("row")
    projected = lax.psum_scatter(
        dot(current, deposit_maps, (0, 0)), "row", scatter_dimension=0, tiled=True
    )
    return current * math.sqrt(total_rows), projected


def on_device(deposit_maps, test_matrix):
    n_row, n_col = lax.axis_size("row"), lax.axis_size("col")
    rows, depth = deposit_maps.shape
    size = test_matrix.shape[1]
    fits = (
        n_col == 4
        and n_row % 4 == 0
        and rows % (n_col * 16) == 0
        and depth % (n_row * 128) == 0
        and size % (n_row * 8) == 0
        and size % 128 == 0
        and depth % (PIECES * 128) == 0
        and rows * n_row * size * 4 <= 4 * 2**20
        and depth * rows * 4 <= 4 * 2**20
        and depth * size * 4 <= 4 * 2**20
    )
    if fits:
        return gathered(deposit_maps, test_matrix)
    return summed(deposit_maps, test_matrix)


def solution(mesh):
    placed = (P("row", "col"), P("col", None))
    return jax.shard_map(
        on_device,
        mesh=mesh,
        in_specs=placed,
        out_specs=(P("row", None), P("row", "col")),
        check_vma=False,
    )
```

```python
import functools
import math

import jax
import jax.numpy as jnp
from jax import lax
from jax.experimental import pallas as pl
from jax.experimental.pallas import tpu as pltpu
from jax.sharding import PartitionSpec as P

MESH = pl.DeviceIdType.MESH
VMEM = pl.BlockSpec(memory_space=pltpu.VMEM)
BLOCK = 64
PIECES = 4
THREE = lax.Precision.HIGH


def dot(left, right, contract, precision=lax.Precision.HIGHEST):
    return lax.dot_general(
        left,
        right,
        ((contract[:1], contract[1:]), ((), ())),
        preferred_element_type=jnp.float32,
        precision=precision,
    )


def small_inverse(block):
    b = block.shape[0]
    row_index = lax.broadcasted_iota(jnp.int32, (b, 128), 0)
    lane = lax.broadcasted_iota(jnp.int32, (b, 128), 1)
    work = jnp.where(lane < b, block, jnp.where(lane == row_index + b, 1.0, 0.0))
    tiles = [work[8 * t : 8 * t + 8, :] for t in range(b // 8)]
    row_index = lax.broadcasted_iota(jnp.int32, (8, 128), 0)
    finished = []
    for group in range(b // 8):
        head, below = tiles[0], tiles[1:]
        first = 8 * group
        wide = [
            [jnp.broadcast_to(tile[:, first + m : first + m + 1], (8, 128)) for m in range(8)]
            for tile in tiles
        ]
        entry = {
            (i, j): jnp.broadcast_to(wide[0][j][i : i + 1, :], (8, 128))
            for i in range(8)
            for j in range(i + 1)
        }
        rows = [jnp.broadcast_to(head[i : i + 1, :], (8, 128)) for i in range(8)]
        pivots = jnp.ones((8, 128), jnp.float32)
        for m in range(8):
            pivot = entry[m, m]
            over = 1.0 / pivot
            for i in range(m + 1, 8):
                factor = entry[i, m] * over
                for j in range(m + 1, i + 1):
                    entry[i, j] = entry[i, j] - factor * entry[j, m]
                rows[i] = rows[i] - factor * rows[m]
                for columns in wide[1:]:
                    columns[i] = columns[i] - factor * columns[m]
            for t in range(len(below)):
                below[t] = below[t] - (wide[t + 1][m] * over) * rows[m]
            pivots = jnp.where(row_index == m, pivot, pivots)
        merged = rows[0]
        for m in range(1, 8):
            merged = jnp.where(row_index == m, rows[m], merged)
        finished.append(merged * lax.rsqrt(pivots))
        tiles = below
    return jnp.concatenate(finished, axis=0)[:, b : 2 * b]


def factor_inverse(x_ref):
    size = x_ref.shape[0]
    lane = lax.broadcasted_iota(jnp.int32, (BLOCK, size), 1)
    row_index = lax.broadcasted_iota(jnp.int32, (BLOCK, size), 0)
    all_rows = lax.broadcasted_iota(jnp.int32, (size, size), 0)
    all_lanes = lax.broadcasted_iota(jnp.int32, (size, size), 1)

    def step(i, carry):
        start = pl.multiple_of(i * BLOCK, BLOCK)
        rows = x_ref[pl.ds(start, BLOCK), :]
        diagonal = pltpu.roll(rows, lax.rem(size - start, size), 1)[:, :128]
        inverse = small_inverse(diagonal)
        inside = (lane >= start) & (lane < start + BLOCK)
        rows = jnp.where(inside, jnp.where(lane == start + row_index, 1.0, 0.0), rows)
        done = dot(inverse, rows, (1, 0))
        upper = jnp.where(lane >= start + BLOCK, done, 0.0)
        update = dot(upper, done, (0, 0))
        below = all_rows >= start + BLOCK
        cleared = (all_lanes >= start) & (all_lanes < start + BLOCK)
        x_ref[...] = jnp.where(below & cleared, 0.0, x_ref[...]) - update
        x_ref[pl.ds(start, BLOCK), :] = done
        return carry

    lax.fori_loop(0, size // BLOCK, step, 0)
    x_ref[...] = jnp.where(all_lanes <= all_rows, x_ref[...], 0.0)


def first_pass_kernel(
    dims, maps_hbm, test_hbm, basis_ref, gram_ref, proj_ref,
    maps_ref, test_ref, load, part, landed, sketch, columns, factor,
    col_send, col_recv, z_send, z_recv, xy_send, xy_recv, core_send, core_recv, a_send, a_recv,
    relay, x_send, x_recv,
):
    n_row, n_col, n_z = dims
    r, c = lax.axis_index("row"), lax.axis_index("col")
    z, x = r // 2, lax.rem(r, 2)
    y, core = c // 2, lax.rem(c, 2)
    width = columns.shape[-1]
    size = factor.shape[0]

    def device(z_to, x_to, y_to, core_to):
        return (z_to * 2 + x_to, y_to * 2 + core_to)

    pieces = load.shape[0]
    depth = maps_ref.shape[-1]
    step = depth // pieces
    loads = []
    for k in range(pieces):
        span = pl.ds(k * step, step)
        loads.append((
            pltpu.make_async_copy(
                maps_hbm.at[:, :, :, span], maps_ref.at[:, :, :, span], load.at[k, 0]
            ),
            pltpu.make_async_copy(test_hbm.at[span], test_ref.at[span], load.at[k, 1]),
        ))
        for copy in loads[-1]:
            copy.start()

    barrier = pltpu.get_barrier_semaphore()
    for k in range(1, n_row):
        pl.semaphore_signal(
            barrier, inc=1, device_id=(lax.rem(r + k, n_row), c), device_id_type=MESH
        )
    for k in range(1, n_col):
        pl.semaphore_signal(
            barrier, inc=1, device_id=(r, lax.rem(c + k, n_col)), device_id_type=MESH
        )

    def send(source, target, send_sem, recv_sem, to):
        copy = pltpu.make_async_remote_copy(
            src_ref=source, dst_ref=target, send_sem=send_sem, recv_sem=recv_sem,
            device_id=to, device_id_type=MESH,
        )
        copy.start()
        return copy

    def share(z_to, x_to):
        start = pl.multiple_of((z_to * 2 + x_to) * width, width)
        return maps_ref.at[:, :, :, pl.ds(start, width)]

    x_peer, y_peer = device(z, 1 - x, y, core), device(z, x, 1 - y, core)
    x_copies, z_copies = [], []

    def exchange_x():
        for d in list(range(1, n_z)) + [0]:
            target = relay.at[d - 1] if d else columns.at[:, :, x, z]
            x_copies.append(
                send(
                    share(lax.rem(z + d, n_z), 1 - x), target,
                    x_send.at[d], x_recv.at[d], x_peer,
                )
            )

    def exchange_z(distances, passed_on):
        for d in distances:
            z_to = lax.rem(z + d, n_z)
            source = relay.at[d - 1] if passed_on else share(z_to, x)
            k = d - 1 + (n_z - 1 if passed_on else 0)
            from_x = 1 - x if passed_on else x
            z_copies.append(
                send(
                    source, columns.at[:, :, from_x, z],
                    a_send.at[k], a_recv.at[k], device(z_to, x, y, core),
                )
            )

    far = n_z // 2
    others = [d for d in range(1, n_z) if d != far]
    sub = part.shape[1]
    partial = None
    for copy, _ in loads:
        copy.wait()
    for k in range(pieces):
        if k == pieces // 2:
            pl.semaphore_wait(barrier, n_row - 1 + n_col - 1)
            exchange_z([far], False)
            exchange_x()
        loads[k][1].wait()
        span = pl.ds(k * step, step)
        term = dot(maps_ref[:, :, :, span].reshape(n_col * sub, step), test_ref[span], (1, 0))
        partial = term if partial is None else partial + term
    part[...] = partial.reshape(part.shape)
    copies = []
    for k in range(1, n_col):
        to = lax.rem(c + k, n_col)
        copies.append(
            send(part.at[to], landed.at[k - 1], col_send.at[k - 1], col_recv.at[k - 1], (r, to))
        )
    total = part[c]
    for k, copy in enumerate(copies):
        copy.wait_recv()
        total = total + landed[k]
    sketch[y, core, x, z] = total
    sent = list(copies)

    copies = []
    for k in range(1, n_z):
        mine = sketch.at[y, core, x, z]
        to = device(lax.rem(z + k, n_z), x, y, core)
        copies.append(send(mine, mine, z_send.at[k - 1], z_recv.at[k - 1], to))
    for copy in copies:
        copy.wait_recv()
    sent += copies

    half = n_z // 2
    low, high = pl.ds(0, half), pl.ds(half, half)
    a = sketch.at[y, core, x, low]
    b = sketch.at[y, core, x, high]
    copies = [
        send(a, a, xy_send.at[0], xy_recv.at[0], x_peer),
        send(b, b, xy_send.at[1], xy_recv.at[1], y_peer),
    ]
    exchange_z(others, False)
    for copy in copies:
        copy.wait_recv()
    sent += copies
    a = sketch.at[y, core, :, low]
    b = sketch.at[:, core, x, high]
    copies = [
        send(a, a, xy_send.at[2], xy_recv.at[2], y_peer),
        send(b, b, xy_send.at[3], xy_recv.at[3], x_peer),
    ]
    for d in [far] + others:
        x_copies[d - 1].wait_recv()
        exchange_z([d], True)
    for copy in copies:
        copy.wait_recv()
    sent += copies

    mine = sketch.at[:, core]
    core_copy = send(mine, mine, core_send, core_recv, device(z, x, y, 1 - core))
    sent.append(core_copy)
    columns[:, :, x, z] = share(z, x)[...]

    def half_gram(which):
        half_sum = None
        for i in range(n_col // 2):
            rows = sketch[i, which].reshape(-1, size)
            term = dot(rows, rows, (0, 0))
            half_sum = term if half_sum is None else half_sum + term
        return half_sum

    gram = half_gram(core)
    core_copy.wait_recv()
    gram = gram + half_gram(1 - core)
    chunks = [(i, j) for i in range(n_col // 2) for j in range(2)]
    factor[...] = gram
    factor_inverse(factor)
    inverse = factor[...]
    for copy in sent + x_copies:
        copy.wait_send()
    gram = None
    for i, j in chunks:
        rows = dot(sketch[i, j].reshape(-1, size), inverse, (1, 1))
        sketch[i, j] = rows.reshape(sketch.shape[2:])
        term = dot(rows, rows, (0, 0), THREE)
        gram = term if gram is None else gram + term
    gram_ref[...] = gram
    basis_ref[...] = sketch[:, :, x, z]
    x_copies[-1].wait_recv()
    for copy in z_copies:
        copy.wait()
    proj = None
    for i, j in chunks:
        term = dot(
            sketch[i, j].reshape(-1, size), columns[i, j].reshape(-1, width), (0, 0),
            THREE,
        )
        proj = term if proj is None else proj + term
    proj_ref[...] = proj


def second_pass_kernel(total_rows, gram_ref, basis_ref, proj_ref, scaled_ref, out_ref, factor):
    size = gram_ref.shape[0]
    row_index = lax.broadcasted_iota(jnp.int32, (size, size), 0)
    lane = lax.broadcasted_iota(jnp.int32, (size, size), 1)
    identity = jnp.where(row_index == lane, 1.0, 0.0)
    weight = jnp.where(lane < row_index, 1.0, 0.5 * identity)
    gram = gram_ref[...]
    error = gram - identity
    small = jnp.sum(error * error) <= 4e-4

    @pl.when(small)
    def _():
        inverse = identity - weight * error
        left = error - dot(weight * error, gram, (1, 0))
        residual = left - dot(identity + left, weight * error, (1, 1))
        factor[...] = inverse - dot(weight * residual, inverse, (1, 0))

    @pl.when(jnp.logical_not(small))
    def _():
        factor[...] = gram
        factor_inverse(factor)

    inverse = factor[...]
    scaled_ref[...] = dot(basis_ref[...], inverse, (1, 1), THREE) * math.sqrt(total_rows)
    out_ref[...] = dot(inverse, proj_ref[...], (1, 0), THREE)


def spread_kernel(n_row, proj_ref, out_ref, send_sem, recv_sem):
    r, c = lax.axis_index("row"), lax.axis_index("col")
    width = proj_ref.shape[-1]
    barrier = pltpu.get_barrier_semaphore()
    for k in range(1, n_row):
        pl.semaphore_signal(
            barrier, inc=1, device_id=(lax.rem(r + k, n_row), c), device_id_type=MESH
        )
    share = pl.ds(pl.multiple_of(r * width, width), width)
    out_ref[:, share] = proj_ref[r]
    pl.semaphore_wait(barrier, n_row - 1)
    copies = []
    for k in range(1, n_row):
        to = lax.rem(r + k, n_row)
        copy = pltpu.make_async_remote_copy(
            src_ref=proj_ref.at[to], dst_ref=out_ref.at[:, share],
            send_sem=send_sem.at[k - 1], recv_sem=recv_sem.at[k - 1],
            device_id=(to, c), device_id_type=MESH,
        )
        copy.start()
        copies.append(copy)
    for copy in copies:
        copy.wait()


def gathered(deposit_maps, test_matrix):
    n_row, n_col = lax.axis_size("row"), lax.axis_size("col")
    rows, depth = deposit_maps.shape
    size = test_matrix.shape[1]
    sub, width, n_z = rows // n_col, depth // n_row, n_row // 2
    f32 = jnp.float32
    maps = deposit_maps.reshape(n_col // 2, 2, sub, depth)
    dma = pltpu.SemaphoreType.DMA
    basis, gram, proj = pl.pallas_call(
        functools.partial(first_pass_kernel, (n_row, n_col, n_z)),
        out_shape=(
            jax.ShapeDtypeStruct((n_col // 2, 2, sub, size), f32),
            jax.ShapeDtypeStruct((size, size), f32),
            jax.ShapeDtypeStruct((size, width), f32),
        ),
        in_specs=[pl.BlockSpec(memory_space=pltpu.HBM)] * 2,
        out_specs=(VMEM, VMEM, VMEM),
        scratch_shapes=[
            pltpu.VMEM(maps.shape, f32),
            pltpu.VMEM(test_matrix.shape, f32),
            dma((PIECES, 2)),
            pltpu.VMEM((n_col, sub, size), f32),
            pltpu.VMEM((n_col - 1, sub, size), f32),
            pltpu.VMEM((n_col // 2, 2, 2, n_z, sub, size), f32),
            pltpu.VMEM((n_col // 2, 2, 2, n_z, sub, width), f32),
            pltpu.VMEM((size, size), f32),
            dma((n_col - 1,)), dma((n_col - 1,)),
            dma((n_z - 1,)), dma((n_z - 1,)),
            dma((4,)), dma((4,)),
            dma, dma,
            dma((2 * n_z - 2,)), dma((2 * n_z - 2,)),
            pltpu.VMEM((n_z - 1, n_col // 2, 2, sub, width), f32),
            dma((n_z,)), dma((n_z,)),
        ],
        compiler_params=pltpu.CompilerParams(
            collective_id=0, has_side_effects=True, vmem_limit_bytes=53 * 2**20
        ),
    )(maps, test_matrix)
    scaled, full = pl.pallas_call(
        functools.partial(second_pass_kernel, rows * n_row),
        out_shape=(
            jax.ShapeDtypeStruct((rows, size), f32),
            jax.ShapeDtypeStruct((size, width), f32),
        ),
        in_specs=[VMEM, VMEM, VMEM],
        out_specs=(VMEM, VMEM),
        scratch_shapes=[pltpu.VMEM((size, size), f32)],
        compiler_params=pltpu.CompilerParams(vmem_limit_bytes=32 * 2**20),
    )(gram, basis.reshape(rows, size), proj)
    projected = pl.pallas_call(
        functools.partial(spread_kernel, n_row),
        out_shape=jax.ShapeDtypeStruct((size // n_row, depth), f32),
        in_specs=[VMEM],
        out_specs=VMEM,
        scratch_shapes=[dma((n_row - 1,)), dma((n_row - 1,))],
        compiler_params=pltpu.CompilerParams(
            collective_id=1, has_side_effects=True, vmem_limit_bytes=32 * 2**20
        ),
    )(full.reshape(n_row, size // n_row, width))
    return scaled, projected


def apply_factor(current, gram_matrix):
    lower_factor = jnp.linalg.cholesky(gram_matrix)
    identity = jnp.eye(gram_matrix.shape[0], dtype=jnp.float32)
    inverse = jax.scipy.linalg.solve_triangular(lower_factor, identity, lower=True)
    return dot(current, inverse, (1, 1))


def summed(deposit_maps, test_matrix):
    current = lax.psum(dot(deposit_maps, test_matrix, (1, 0)), "col")
    for _ in range(2):
        gram_matrix = lax.psum(dot(current, current, (0, 0)), "row")
        current = apply_factor(current, gram_matrix)
    total_rows = current.shape[0] * lax.axis_size("row")
    projected = lax.psum_scatter(
        dot(current, deposit_maps, (0, 0)), "row", scatter_dimension=0, tiled=True
    )
    return current * math.sqrt(total_rows), projected


def on_device(deposit_maps, test_matrix):
    n_row, n_col = lax.axis_size("row"), lax.axis_size("col")
    rows, depth = deposit_maps.shape
    size = test_matrix.shape[1]
    fits = (
        n_col == 4
        and n_row % 4 == 0
        and rows % (n_col * 16) == 0
        and depth % (n_row * 128) == 0
        and size % (n_row * 8) == 0
        and size % 128 == 0
        and depth % (PIECES * 128) == 0
        and rows * n_row * size * 4 <= 4 * 2**20
        and depth * rows * 4 <= 4 * 2**20
        and depth * size * 4 <= 4 * 2**20
    )
    if fits:
        return gathered(deposit_maps, test_matrix)
    return summed(deposit_maps, test_matrix)


def solution(mesh):
    placed = (P("row", "col"), P("col", None))
    return jax.shard_map(
        on_device,
        mesh=mesh,
        in_specs=placed,
        out_specs=(P("row", None), P("row", "col")),
        check_vma=False,
    )
```

```python
import functools
import math

import jax
import jax.numpy as jnp
from jax import lax
from jax.experimental import pallas as pl
from jax.experimental.pallas import tpu as pltpu
from jax.sharding import PartitionSpec as P

MESH = pl.DeviceIdType.MESH
VMEM = pl.BlockSpec(memory_space=pltpu.VMEM)
BLOCK = 64
PIECES = 4
THREE = lax.Precision.HIGH


def dot(left, right, contract, precision=lax.Precision.HIGHEST):
    return lax.dot_general(
        left,
        right,
        ((contract[:1], contract[1:]), ((), ())),
        preferred_element_type=jnp.float32,
        precision=precision,
    )


def small_inverse(block):
    b = block.shape[0]
    row_index = lax.broadcasted_iota(jnp.int32, (b, 128), 0)
    lane = lax.broadcasted_iota(jnp.int32, (b, 128), 1)
    work = jnp.where(lane < b, block, jnp.where(lane == row_index + b, 1.0, 0.0))
    tiles = [work[8 * t : 8 * t + 8, :] for t in range(b // 8)]
    row_index = lax.broadcasted_iota(jnp.int32, (8, 128), 0)
    finished = []
    for group in range(b // 8):
        head, below = tiles[0], tiles[1:]
        first = 8 * group
        wide = [
            [jnp.broadcast_to(tile[:, first + m : first + m + 1], (8, 128)) for m in range(8)]
            for tile in tiles
        ]
        entry = {
            (i, j): jnp.broadcast_to(wide[0][j][i : i + 1, :], (8, 128))
            for i in range(8)
            for j in range(i + 1)
        }
        rows = [jnp.broadcast_to(head[i : i + 1, :], (8, 128)) for i in range(8)]
        pivots = jnp.ones((8, 128), jnp.float32)
        for m in range(8):
            pivot = entry[m, m]
            over = 1.0 / pivot
            for i in range(m + 1, 8):
                factor = entry[i, m] * over
                for j in range(m + 1, i + 1):
                    entry[i, j] = entry[i, j] - factor * entry[j, m]
                rows[i] = rows[i] - factor * rows[m]
                for columns in wide[1:]:
                    columns[i] = columns[i] - factor * columns[m]
            for t in range(len(below)):
                below[t] = below[t] - (wide[t + 1][m] * over) * rows[m]
            pivots = jnp.where(row_index == m, pivot, pivots)
        merged = rows[0]
        for m in range(1, 8):
            merged = jnp.where(row_index == m, rows[m], merged)
        finished.append(merged * lax.rsqrt(pivots))
        tiles = below
    return jnp.concatenate(finished, axis=0)[:, b : 2 * b]


def factor_inverse(x_ref):
    size = x_ref.shape[0]
    lane = lax.broadcasted_iota(jnp.int32, (BLOCK, size), 1)
    row_index = lax.broadcasted_iota(jnp.int32, (BLOCK, size), 0)
    for start in range(0, size, BLOCK):
        end = start + BLOCK
        rows = x_ref[start:end, :]
        diagonal = (pltpu.roll(rows, size - start, 1) if start else rows)[:, :128]
        inverse = small_inverse(diagonal)
        inside = (lane >= start) & (lane < end)
        rows = jnp.where(inside, jnp.where(lane == start + row_index, 1.0, 0.0), rows)
        done = dot(inverse, rows, (1, 0))
        if end < size:
            low = end // 128 * 128
            upper = jnp.where(lane >= end, done, 0.0)[:, low:]
            update = dot(upper, done, (0, 0))
            rest_rows = low + lax.broadcasted_iota(jnp.int32, update.shape, 0)
            rest_lanes = lax.broadcasted_iota(jnp.int32, update.shape, 1)
            cleared = (rest_rows >= end) & (rest_lanes >= start) & (rest_lanes < end)
            x_ref[low:, :] = jnp.where(cleared, 0.0, x_ref[low:, :]) - update
        x_ref[start:end, :] = jnp.where(lane <= start + row_index, done, 0.0)


def first_pass_kernel(
    dims, maps_hbm, test_hbm, basis_ref, gram_ref, proj_ref,
    maps_ref, test_ref, load, part, landed, sketch, columns, factor,
    col_send, col_recv, z_send, z_recv, xy_send, xy_recv, core_send, core_recv, a_send, a_recv,
    relay, x_send, x_recv,
):
    n_row, n_col, n_z = dims
    r, c = lax.axis_index("row"), lax.axis_index("col")
    z, x = r // 2, lax.rem(r, 2)
    y, core = c // 2, lax.rem(c, 2)
    width = columns.shape[-1]
    size = factor.shape[0]

    def device(z_to, x_to, y_to, core_to):
        return (z_to * 2 + x_to, y_to * 2 + core_to)

    pieces = load.shape[0]
    depth = maps_ref.shape[-1]
    step = depth // pieces
    loads = []
    for k in range(pieces):
        span = pl.ds(k * step, step)
        loads.append((
            pltpu.make_async_copy(
                maps_hbm.at[:, :, :, span], maps_ref.at[:, :, :, span], load.at[k, 0]
            ),
            pltpu.make_async_copy(test_hbm.at[span], test_ref.at[span], load.at[k, 1]),
        ))
        for copy in loads[-1]:
            copy.start()

    barrier = pltpu.get_barrier_semaphore()
    for k in range(1, n_row):
        pl.semaphore_signal(
            barrier, inc=1, device_id=(lax.rem(r + k, n_row), c), device_id_type=MESH
        )
    for k in range(1, n_col):
        pl.semaphore_signal(
            barrier, inc=1, device_id=(r, lax.rem(c + k, n_col)), device_id_type=MESH
        )

    def send(source, target, send_sem, recv_sem, to):
        copy = pltpu.make_async_remote_copy(
            src_ref=source, dst_ref=target, send_sem=send_sem, recv_sem=recv_sem,
            device_id=to, device_id_type=MESH,
        )
        copy.start()
        return copy

    def share(z_to, x_to):
        start = pl.multiple_of((z_to * 2 + x_to) * width, width)
        return maps_ref.at[:, :, :, pl.ds(start, width)]

    x_peer, y_peer = device(z, 1 - x, y, core), device(z, x, 1 - y, core)
    x_copies, z_copies = [], []

    def exchange_x():
        for d in list(range(1, n_z)) + [0]:
            target = relay.at[d - 1] if d else columns.at[:, :, x, z]
            x_copies.append(
                send(
                    share(lax.rem(z + d, n_z), 1 - x), target,
                    x_send.at[d], x_recv.at[d], x_peer,
                )
            )

    def exchange_z(distances, passed_on):
        for d in distances:
            z_to = lax.rem(z + d, n_z)
            source = relay.at[d - 1] if passed_on else share(z_to, x)
            k = d - 1 + (n_z - 1 if passed_on else 0)
            from_x = 1 - x if passed_on else x
            z_copies.append(
                send(
                    source, columns.at[:, :, from_x, z],
                    a_send.at[k], a_recv.at[k], device(z_to, x, y, core),
                )
            )

    far = n_z // 2
    others = [d for d in range(1, n_z) if d != far]
    sub = part.shape[1]
    partial = None
    for copy, _ in loads:
        copy.wait()
    for k in range(pieces):
        if k == pieces // 2:
            pl.semaphore_wait(barrier, n_row - 1 + n_col - 1)
            exchange_z([far], False)
            exchange_x()
        loads[k][1].wait()
        span = pl.ds(k * step, step)
        term = dot(maps_ref[:, :, :, span].reshape(n_col * sub, step), test_ref[span], (1, 0))
        partial = term if partial is None else partial + term
    part[...] = partial.reshape(part.shape)
    copies = []
    for k in range(1, n_col):
        to = lax.rem(c + k, n_col)
        copies.append(
            send(part.at[to], landed.at[k - 1], col_send.at[k - 1], col_recv.at[k - 1], (r, to))
        )
    total = part[c]
    for k, copy in enumerate(copies):
        copy.wait_recv()
        total = total + landed[k]
    sketch[y, core, x, z] = total
    sent = list(copies)

    copies = []
    for k in range(1, n_z):
        mine = sketch.at[y, core, x, z]
        to = device(lax.rem(z + k, n_z), x, y, core)
        copies.append(send(mine, mine, z_send.at[k - 1], z_recv.at[k - 1], to))
    for copy in copies:
        copy.wait_recv()
    sent += copies

    half = n_z // 2
    low, high = pl.ds(0, half), pl.ds(half, half)
    a = sketch.at[y, core, x, low]
    b = sketch.at[y, core, x, high]
    copies = [
        send(a, a, xy_send.at[0], xy_recv.at[0], x_peer),
        send(b, b, xy_send.at[1], xy_recv.at[1], y_peer),
    ]
    exchange_z(others, False)
    for copy in copies:
        copy.wait_recv()
    sent += copies
    a = sketch.at[y, core, :, low]
    b = sketch.at[:, core, x, high]
    copies = [
        send(a, a, xy_send.at[2], xy_recv.at[2], y_peer),
        send(b, b, xy_send.at[3], xy_recv.at[3], x_peer),
    ]
    for d in [far] + others:
        x_copies[d - 1].wait_recv()
        exchange_z([d], True)
    for copy in copies:
        copy.wait_recv()
    sent += copies

    mine = sketch.at[:, core]
    core_copy = send(mine, mine, core_send, core_recv, device(z, x, y, 1 - core))
    sent.append(core_copy)
    columns[:, :, x, z] = share(z, x)[...]

    def half_gram(which):
        half_sum = None
        for i in range(n_col // 2):
            rows = sketch[i, which].reshape(-1, size)
            term = dot(rows, rows, (0, 0))
            half_sum = term if half_sum is None else half_sum + term
        return half_sum

    gram = half_gram(core)
    core_copy.wait_recv()
    gram = gram + half_gram(1 - core)
    chunks = [(i, j) for i in range(n_col // 2) for j in range(2)]
    factor[...] = gram
    factor_inverse(factor)
    inverse = factor[...]
    for copy in sent + x_copies:
        copy.wait_send()
    x_copies[-1].wait_recv()
    for copy in z_copies:
        copy.wait()
    both = None
    for i, j in chunks:
        rows = dot(sketch[i, j].reshape(-1, size), inverse, (1, 1))
        sketch[i, j] = rows.reshape(sketch.shape[2:])
        wide = jnp.concatenate([rows, columns[i, j].reshape(-1, width)], axis=1)
        term = dot(rows, wide, (0, 0), THREE)
        both = term if both is None else both + term
    gram_ref[...] = both[:, :size]
    proj_ref[...] = both[:, size:]
    basis_ref[...] = sketch[:, :, x, z]


def second_pass_kernel(total_rows, gram_ref, basis_ref, proj_ref, scaled_ref, out_ref, factor):
    size = gram_ref.shape[0]
    row_index = lax.broadcasted_iota(jnp.int32, (size, size), 0)
    lane = lax.broadcasted_iota(jnp.int32, (size, size), 1)
    identity = jnp.where(row_index == lane, 1.0, 0.0)
    weight = jnp.where(lane < row_index, 1.0, 0.5 * identity)
    gram = gram_ref[...]
    error = gram - identity
    small = jnp.sum(error * error) <= 4e-4

    @pl.when(small)
    def _():
        inverse = identity - weight * error
        left = error - dot(weight * error, gram, (1, 0))
        residual = left - dot(identity + left, weight * error, (1, 1))
        factor[...] = inverse - dot(weight * residual, inverse, (1, 0))

    @pl.when(jnp.logical_not(small))
    def _():
        factor[...] = gram
        factor_inverse(factor)

    inverse = factor[...]
    scaled_ref[...] = dot(basis_ref[...], inverse, (1, 1), THREE) * math.sqrt(total_rows)
    out_ref[...] = dot(inverse, proj_ref[...], (1, 0), THREE)


def spread_kernel(n_row, proj_ref, out_ref, send_sem, recv_sem):
    r, c = lax.axis_index("row"), lax.axis_index("col")
    width = proj_ref.shape[-1]
    barrier = pltpu.get_barrier_semaphore()
    for k in range(1, n_row):
        pl.semaphore_signal(
            barrier, inc=1, device_id=(lax.rem(r + k, n_row), c), device_id_type=MESH
        )
    share = pl.ds(pl.multiple_of(r * width, width), width)
    out_ref[:, share] = proj_ref[r]
    pl.semaphore_wait(barrier, n_row - 1)
    copies = []
    for k in sorted(range(1, n_row), key=lambda step: abs(step - n_row // 2)):
        to = lax.rem(r + k, n_row)
        copy = pltpu.make_async_remote_copy(
            src_ref=proj_ref.at[to], dst_ref=out_ref.at[:, share],
            send_sem=send_sem.at[k - 1], recv_sem=recv_sem.at[k - 1],
            device_id=(to, c), device_id_type=MESH,
        )
        copy.start()
        copies.append(copy)
    for copy in copies:
        copy.wait()


def gathered(deposit_maps, test_matrix):
    n_row, n_col = lax.axis_size("row"), lax.axis_size("col")
    rows, depth = deposit_maps.shape
    size = test_matrix.shape[1]
    sub, width, n_z = rows // n_col, depth // n_row, n_row // 2
    f32 = jnp.float32
    maps = deposit_maps.reshape(n_col // 2, 2, sub, depth)
    dma = pltpu.SemaphoreType.DMA
    basis, gram, proj = pl.pallas_call(
        functools.partial(first_pass_kernel, (n_row, n_col, n_z)),
        out_shape=(
            jax.ShapeDtypeStruct((n_col // 2, 2, sub, size), f32),
            jax.ShapeDtypeStruct((size, size), f32),
            jax.ShapeDtypeStruct((size, width), f32),
        ),
        in_specs=[pl.BlockSpec(memory_space=pltpu.HBM)] * 2,
        out_specs=(VMEM, VMEM, VMEM),
        scratch_shapes=[
            pltpu.VMEM(maps.shape, f32),
            pltpu.VMEM(test_matrix.shape, f32),
            dma((PIECES, 2)),
            pltpu.VMEM((n_col, sub, size), f32),
            pltpu.VMEM((n_col - 1, sub, size), f32),
            pltpu.VMEM((n_col // 2, 2, 2, n_z, sub, size), f32),
            pltpu.VMEM((n_col // 2, 2, 2, n_z, sub, width), f32),
            pltpu.VMEM((size, size), f32),
            dma((n_col - 1,)), dma((n_col - 1,)),
            dma((n_z - 1,)), dma((n_z - 1,)),
            dma((4,)), dma((4,)),
            dma, dma,
            dma((2 * n_z - 2,)), dma((2 * n_z - 2,)),
            pltpu.VMEM((n_z - 1, n_col // 2, 2, sub, width), f32),
            dma((n_z,)), dma((n_z,)),
        ],
        compiler_params=pltpu.CompilerParams(
            collective_id=0, has_side_effects=True, vmem_limit_bytes=53 * 2**20
        ),
    )(maps, test_matrix)
    scaled, full = pl.pallas_call(
        functools.partial(second_pass_kernel, rows * n_row),
        out_shape=(
            jax.ShapeDtypeStruct((rows, size), f32),
            jax.ShapeDtypeStruct((size, width), f32),
        ),
        in_specs=[VMEM, VMEM, VMEM],
        out_specs=(VMEM, VMEM),
        scratch_shapes=[pltpu.VMEM((size, size), f32)],
        compiler_params=pltpu.CompilerParams(vmem_limit_bytes=32 * 2**20),
    )(gram, basis.reshape(rows, size), proj)
    projected = pl.pallas_call(
        functools.partial(spread_kernel, n_row),
        out_shape=jax.ShapeDtypeStruct((size // n_row, depth), f32),
        in_specs=[VMEM],
        out_specs=VMEM,
        scratch_shapes=[dma((n_row - 1,)), dma((n_row - 1,))],
        compiler_params=pltpu.CompilerParams(
            collective_id=1, has_side_effects=True, vmem_limit_bytes=32 * 2**20
        ),
    )(full.reshape(n_row, size // n_row, width))
    return scaled, projected


def apply_factor(current, gram_matrix):
    lower_factor = jnp.linalg.cholesky(gram_matrix)
    identity = jnp.eye(gram_matrix.shape[0], dtype=jnp.float32)
    inverse = jax.scipy.linalg.solve_triangular(lower_factor, identity, lower=True)
    return dot(current, inverse, (1, 1))


def summed(deposit_maps, test_matrix):
    current = lax.psum(dot(deposit_maps, test_matrix, (1, 0)), "col")
    for _ in range(2):
        gram_matrix = lax.psum(dot(current, current, (0, 0)), "row")
        current = apply_factor(current, gram_matrix)
    total_rows = current.shape[0] * lax.axis_size("row")
    projected = lax.psum_scatter(
        dot(current, deposit_maps, (0, 0)), "row", scatter_dimension=0, tiled=True
    )
    return current * math.sqrt(total_rows), projected


def on_device(deposit_maps, test_matrix):
    n_row, n_col = lax.axis_size("row"), lax.axis_size("col")
    rows, depth = deposit_maps.shape
    size = test_matrix.shape[1]
    fits = (
        n_col == 4
        and n_row % 4 == 0
        and rows % (n_col * 16) == 0
        and depth % (n_row * 128) == 0
        and size % (n_row * 8) == 0
        and size % 128 == 0
        and depth % (PIECES * 128) == 0
        and rows * n_row * size * 4 <= 4 * 2**20
        and depth * rows * 4 <= 4 * 2**20
        and depth * size * 4 <= 4 * 2**20
    )
    if fits:
        return gathered(deposit_maps, test_matrix)
    return summed(deposit_maps, test_matrix)


def solution(mesh):
    placed = (P("row", "col"), P("col", None))
    return jax.shard_map(
        on_device,
        mesh=mesh,
        in_specs=placed,
        out_specs=(P("row", None), P("row", "col")),
        check_vma=False,
    )
```

```python
import functools
import math

import jax
import jax.numpy as jnp
from jax import lax
from jax.experimental import pallas as pl
from jax.experimental.pallas import tpu as pltpu
from jax.sharding import PartitionSpec as P

MESH = pl.DeviceIdType.MESH
VMEM = pl.BlockSpec(memory_space=pltpu.VMEM)
BLOCK = 64
PIECES = 4
THREE = lax.Precision.HIGH


def dot(left, right, contract, precision=lax.Precision.HIGHEST):
    return lax.dot_general(
        left,
        right,
        ((contract[:1], contract[1:]), ((), ())),
        preferred_element_type=jnp.float32,
        precision=precision,
    )


def small_inverse(block):
    b = block.shape[0]
    row_index = lax.broadcasted_iota(jnp.int32, (b, 128), 0)
    lane = lax.broadcasted_iota(jnp.int32, (b, 128), 1)
    work = jnp.where(lane < b, block, jnp.where(lane == row_index + b, 1.0, 0.0))
    tiles = [work[8 * t : 8 * t + 8, :] for t in range(b // 8)]
    row_index = lax.broadcasted_iota(jnp.int32, (8, 128), 0)
    finished = []
    for group in range(b // 8):
        head, below = tiles[0], tiles[1:]
        first = 8 * group
        wide = [
            [jnp.broadcast_to(tile[:, first + m : first + m + 1], (8, 128)) for m in range(8)]
            for tile in tiles
        ]
        entry = {
            (i, j): jnp.broadcast_to(wide[0][j][i : i + 1, :], (8, 128))
            for i in range(8)
            for j in range(i + 1)
        }
        rows = [jnp.broadcast_to(head[i : i + 1, :], (8, 128)) for i in range(8)]
        pivots = jnp.ones((8, 128), jnp.float32)
        for m in range(8):
            pivot = entry[m, m]
            over = 1.0 / pivot
            for i in range(m + 1, 8):
                factor = entry[i, m] * over
                for j in range(m + 1, i + 1):
                    entry[i, j] = entry[i, j] - (entry[i, m] * entry[j, m]) * over
                rows[i] = rows[i] - factor * rows[m]
                for columns in wide[1:]:
                    columns[i] = columns[i] - factor * columns[m]
            for t in range(len(below)):
                below[t] = below[t] - (wide[t + 1][m] * over) * rows[m]
            pivots = jnp.where(row_index == m, pivot, pivots)
        merged = rows[0]
        for m in range(1, 8):
            merged = jnp.where(row_index == m, rows[m], merged)
        finished.append(merged * lax.rsqrt(pivots))
        tiles = below
    return jnp.concatenate(finished, axis=0)[:, b : 2 * b]


def factor_inverse(x_ref):
    size = x_ref.shape[0]
    lane = lax.broadcasted_iota(jnp.int32, (BLOCK, size), 1)
    row_index = lax.broadcasted_iota(jnp.int32, (BLOCK, size), 0)
    all_rows = lax.broadcasted_iota(jnp.int32, (size, size), 0)
    all_lanes = lax.broadcasted_iota(jnp.int32, (size, size), 1)

    def step(i, carry):
        start = pl.multiple_of(i * BLOCK, BLOCK)
        rows = x_ref[pl.ds(start, BLOCK), :]
        diagonal = pltpu.roll(rows, lax.rem(size - start, size), 1)[:, :128]
        inverse = small_inverse(diagonal)
        inside = (lane >= start) & (lane < start + BLOCK)
        rows = jnp.where(inside, jnp.where(lane == start + row_index, 1.0, 0.0), rows)
        done = dot(inverse, rows, (1, 0))
        upper = jnp.where(lane >= start + BLOCK, done, 0.0)
        update = dot(upper, done, (0, 0))
        below = all_rows >= start + BLOCK
        cleared = (all_lanes >= start) & (all_lanes < start + BLOCK)
        x_ref[...] = jnp.where(below & cleared, 0.0, x_ref[...]) - update
        x_ref[pl.ds(start, BLOCK), :] = done
        return carry

    lax.fori_loop(0, size // BLOCK, step, 0)
    x_ref[...] = jnp.where(all_lanes <= all_rows, x_ref[...], 0.0)


def first_pass_kernel(
    dims, maps_hbm, test_hbm, basis_ref, gram_ref, proj_ref,
    maps_ref, test_ref, load, part, landed, sketch, columns, factor,
    col_send, col_recv, z_send, z_recv, xy_send, xy_recv, core_send, core_recv, a_send, a_recv,
    relay, x_send, x_recv,
):
    n_row, n_col, n_z = dims
    r, c = lax.axis_index("row"), lax.axis_index("col")
    z, x = r // 2, lax.rem(r, 2)
    y, core = c // 2, lax.rem(c, 2)
    width = columns.shape[-1]
    size = factor.shape[0]

    def device(z_to, x_to, y_to, core_to):
        return (z_to * 2 + x_to, y_to * 2 + core_to)

    pieces = load.shape[0]
    depth = maps_ref.shape[-1]
    step = depth // pieces
    loads = []
    for k in range(pieces):
        span = pl.ds(k * step, step)
        loads.append((
            pltpu.make_async_copy(
                maps_hbm.at[:, :, :, span], maps_ref.at[:, :, :, span], load.at[k, 0]
            ),
            pltpu.make_async_copy(test_hbm.at[span], test_ref.at[span], load.at[k, 1]),
        ))
        for copy in loads[-1]:
            copy.start()

    barrier = pltpu.get_barrier_semaphore()
    for k in range(1, n_row):
        pl.semaphore_signal(
            barrier, inc=1, device_id=(lax.rem(r + k, n_row), c), device_id_type=MESH
        )
    for k in range(1, n_col):
        pl.semaphore_signal(
            barrier, inc=1, device_id=(r, lax.rem(c + k, n_col)), device_id_type=MESH
        )

    def send(source, target, send_sem, recv_sem, to):
        copy = pltpu.make_async_remote_copy(
            src_ref=source, dst_ref=target, send_sem=send_sem, recv_sem=recv_sem,
            device_id=to, device_id_type=MESH,
        )
        copy.start()
        return copy

    def share(z_to, x_to):
        start = pl.multiple_of((z_to * 2 + x_to) * width, width)
        return maps_ref.at[:, :, :, pl.ds(start, width)]

    x_peer, y_peer = device(z, 1 - x, y, core), device(z, x, 1 - y, core)
    x_copies, z_copies = [], []

    def exchange_x():
        for d in list(range(1, n_z)) + [0]:
            target = relay.at[d - 1] if d else columns.at[:, :, x, z]
            x_copies.append(
                send(
                    share(lax.rem(z + d, n_z), 1 - x), target,
                    x_send.at[d], x_recv.at[d], x_peer,
                )
            )

    def exchange_z(distances, passed_on):
        for d in distances:
            z_to = lax.rem(z + d, n_z)
            source = relay.at[d - 1] if passed_on else share(z_to, x)
            k = d - 1 + (n_z - 1 if passed_on else 0)
            from_x = 1 - x if passed_on else x
            z_copies.append(
                send(
                    source, columns.at[:, :, from_x, z],
                    a_send.at[k], a_recv.at[k], device(z_to, x, y, core),
                )
            )

    far = n_z // 2
    others = [d for d in range(1, n_z) if d != far]
    sub = part.shape[1]
    partial = None
    for copy, _ in loads:
        copy.wait()
    for k in range(pieces):
        if k == pieces // 2:
            pl.semaphore_wait(barrier, n_row - 1 + n_col - 1)
            exchange_z([far], False)
            exchange_x()
        loads[k][1].wait()
        span = pl.ds(k * step, step)
        term = dot(maps_ref[:, :, :, span].reshape(n_col * sub, step), test_ref[span], (1, 0))
        partial = term if partial is None else partial + term
    part[...] = partial.reshape(part.shape)
    copies = []
    for k in range(1, n_col):
        to = lax.rem(c + k, n_col)
        copies.append(
            send(part.at[to], landed.at[k - 1], col_send.at[k - 1], col_recv.at[k - 1], (r, to))
        )
    total = part[c]
    for k, copy in enumerate(copies):
        copy.wait_recv()
        total = total + landed[k]
    sketch[y, core, x, z] = total
    sent = list(copies)

    copies = []
    for k in range(1, n_z):
        mine = sketch.at[y, core, x, z]
        to = device(lax.rem(z + k, n_z), x, y, core)
        copies.append(send(mine, mine, z_send.at[k - 1], z_recv.at[k - 1], to))
    for copy in copies:
        copy.wait_recv()
    sent += copies

    half = n_z // 2
    low, high = pl.ds(0, half), pl.ds(half, half)
    a = sketch.at[y, core, x, low]
    b = sketch.at[y, core, x, high]
    copies = [
        send(a, a, xy_send.at[0], xy_recv.at[0], x_peer),
        send(b, b, xy_send.at[1], xy_recv.at[1], y_peer),
    ]
    exchange_z(others, False)
    for copy in copies:
        copy.wait_recv()
    sent += copies
    a = sketch.at[y, core, :, low]
    b = sketch.at[:, core, x, high]
    copies = [
        send(a, a, xy_send.at[2], xy_recv.at[2], y_peer),
        send(b, b, xy_send.at[3], xy_recv.at[3], x_peer),
    ]
    for d in [far] + others:
        x_copies[d - 1].wait_recv()
        exchange_z([d], True)
    for copy in copies:
        copy.wait_recv()
    sent += copies

    mine = sketch.at[:, core]
    core_copy = send(mine, mine, core_send, core_recv, device(z, x, y, 1 - core))
    sent.append(core_copy)
    columns[:, :, x, z] = share(z, x)[...]

    def half_gram(which):
        half_sum = None
        for i in range(n_col // 2):
            rows = sketch[i, which].reshape(-1, size)
            term = dot(rows, rows, (0, 0))
            half_sum = term if half_sum is None else half_sum + term
        return half_sum

    gram = half_gram(core)
    core_copy.wait_recv()
    gram = gram + half_gram(1 - core)
    chunks = [(i, j) for i in range(n_col // 2) for j in range(2)]
    factor[...] = gram
    factor_inverse(factor)
    inverse = factor[...]
    for copy in sent + x_copies:
        copy.wait_send()
    x_copies[-1].wait_recv()
    for copy in z_copies:
        copy.wait()
    both = None
    for i, j in chunks:
        rows = dot(sketch[i, j].reshape(-1, size), inverse, (1, 1))
        sketch[i, j] = rows.reshape(sketch.shape[2:])
        wide = jnp.concatenate([rows, columns[i, j].reshape(-1, width)], axis=1)
        term = dot(rows, wide, (0, 0), THREE)
        both = term if both is None else both + term
    gram_ref[...] = both[:, :size]
    proj_ref[...] = both[:, size:]
    basis_ref[...] = sketch[:, :, x, z]


def second_pass_kernel(total_rows, gram_ref, basis_ref, proj_ref, scaled_ref, out_ref, factor):
    size = gram_ref.shape[0]
    row_index = lax.broadcasted_iota(jnp.int32, (size, size), 0)
    lane = lax.broadcasted_iota(jnp.int32, (size, size), 1)
    identity = jnp.where(row_index == lane, 1.0, 0.0)
    weight = jnp.where(lane < row_index, 1.0, 0.5 * identity)
    gram = gram_ref[...]
    error = gram - identity
    small = jnp.sum(error * error) <= 4e-4

    @pl.when(small)
    def _():
        inverse = identity - weight * error
        left = error - dot(weight * error, gram, (1, 0))
        residual = left - dot(identity + left, weight * error, (1, 1))
        factor[...] = inverse - dot(weight * residual, inverse, (1, 0))

    @pl.when(jnp.logical_not(small))
    def _():
        factor[...] = gram
        factor_inverse(factor)

    inverse = factor[...]
    scaled_ref[...] = dot(basis_ref[...], inverse, (1, 1), THREE) * math.sqrt(total_rows)
    out_ref[...] = dot(inverse, proj_ref[...], (1, 0), THREE)


def spread_kernel(n_row, proj_ref, out_ref, send_sem, recv_sem):
    r, c = lax.axis_index("row"), lax.axis_index("col")
    width = proj_ref.shape[-1]
    barrier = pltpu.get_barrier_semaphore()
    for k in range(1, n_row):
        pl.semaphore_signal(
            barrier, inc=1, device_id=(lax.rem(r + k, n_row), c), device_id_type=MESH
        )
    share = pl.ds(pl.multiple_of(r * width, width), width)
    out_ref[:, share] = proj_ref[r]
    pl.semaphore_wait(barrier, n_row - 1)
    copies = []
    for k in range(1, n_row):
        to = lax.rem(r + k, n_row)
        copy = pltpu.make_async_remote_copy(
            src_ref=proj_ref.at[to], dst_ref=out_ref.at[:, share],
            send_sem=send_sem.at[k - 1], recv_sem=recv_sem.at[k - 1],
            device_id=(to, c), device_id_type=MESH,
        )
        copy.start()
        copies.append(copy)
    for copy in copies:
        copy.wait()


def gathered(deposit_maps, test_matrix):
    n_row, n_col = lax.axis_size("row"), lax.axis_size("col")
    rows, depth = deposit_maps.shape
    size = test_matrix.shape[1]
    sub, width, n_z = rows // n_col, depth // n_row, n_row // 2
    f32 = jnp.float32
    maps = deposit_maps.reshape(n_col // 2, 2, sub, depth)
    dma = pltpu.SemaphoreType.DMA
    basis, gram, proj = pl.pallas_call(
        functools.partial(first_pass_kernel, (n_row, n_col, n_z)),
        out_shape=(
            jax.ShapeDtypeStruct((n_col // 2, 2, sub, size), f32),
            jax.ShapeDtypeStruct((size, size), f32),
            jax.ShapeDtypeStruct((size, width), f32),
        ),
        in_specs=[pl.BlockSpec(memory_space=pltpu.HBM)] * 2,
        out_specs=(VMEM, VMEM, VMEM),
        scratch_shapes=[
            pltpu.VMEM(maps.shape, f32),
            pltpu.VMEM(test_matrix.shape, f32),
            dma((PIECES, 2)),
            pltpu.VMEM((n_col, sub, size), f32),
            pltpu.VMEM((n_col - 1, sub, size), f32),
            pltpu.VMEM((n_col // 2, 2, 2, n_z, sub, size), f32),
            pltpu.VMEM((n_col // 2, 2, 2, n_z, sub, width), f32),
            pltpu.VMEM((size, size), f32),
            dma((n_col - 1,)), dma((n_col - 1,)),
            dma((n_z - 1,)), dma((n_z - 1,)),
            dma((4,)), dma((4,)),
            dma, dma,
            dma((2 * n_z - 2,)), dma((2 * n_z - 2,)),
            pltpu.VMEM((n_z - 1, n_col // 2, 2, sub, width), f32),
            dma((n_z,)), dma((n_z,)),
        ],
        compiler_params=pltpu.CompilerParams(
            collective_id=0, has_side_effects=True, vmem_limit_bytes=53 * 2**20
        ),
    )(maps, test_matrix)
    scaled, full = pl.pallas_call(
        functools.partial(second_pass_kernel, rows * n_row),
        out_shape=(
            jax.ShapeDtypeStruct((rows, size), f32),
            jax.ShapeDtypeStruct((size, width), f32),
        ),
        in_specs=[VMEM, VMEM, VMEM],
        out_specs=(VMEM, VMEM),
        scratch_shapes=[pltpu.VMEM((size, size), f32)],
        compiler_params=pltpu.CompilerParams(vmem_limit_bytes=32 * 2**20),
    )(gram, basis.reshape(rows, size), proj)
    projected = pl.pallas_call(
        functools.partial(spread_kernel, n_row),
        out_shape=jax.ShapeDtypeStruct((size // n_row, depth), f32),
        in_specs=[VMEM],
        out_specs=VMEM,
        scratch_shapes=[dma((n_row - 1,)), dma((n_row - 1,))],
        compiler_params=pltpu.CompilerParams(
            collective_id=1, has_side_effects=True, vmem_limit_bytes=32 * 2**20
        ),
    )(full.reshape(n_row, size // n_row, width))
    return scaled, projected


def apply_factor(current, gram_matrix):
    lower_factor = jnp.linalg.cholesky(gram_matrix)
    identity = jnp.eye(gram_matrix.shape[0], dtype=jnp.float32)
    inverse = jax.scipy.linalg.solve_triangular(lower_factor, identity, lower=True)
    return dot(current, inverse, (1, 1))


def summed(deposit_maps, test_matrix):
    current = lax.psum(dot(deposit_maps, test_matrix, (1, 0)), "col")
    for _ in range(2):
        gram_matrix = lax.psum(dot(current, current, (0, 0)), "row")
        current = apply_factor(current, gram_matrix)
    total_rows = current.shape[0] * lax.axis_size("row")
    projected = lax.psum_scatter(
        dot(current, deposit_maps, (0, 0)), "row", scatter_dimension=0, tiled=True
    )
    return current * math.sqrt(total_rows), projected


def on_device(deposit_maps, test_matrix):
    n_row, n_col = lax.axis_size("row"), lax.axis_size("col")
    rows, depth = deposit_maps.shape
    size = test_matrix.shape[1]
    fits = (
        n_col == 4
        and n_row % 4 == 0
        and rows % (n_col * 16) == 0
        and depth % (n_row * 128) == 0
        and size % (n_row * 8) == 0
        and size % 128 == 0
        and depth % (PIECES * 128) == 0
        and rows * n_row * size * 4 <= 4 * 2**20
        and depth * rows * 4 <= 4 * 2**20
        and depth * size * 4 <= 4 * 2**20
    )
    if fits:
        return gathered(deposit_maps, test_matrix)
    return summed(deposit_maps, test_matrix)


def solution(mesh):
    placed = (P("row", "col"), P("col", None))
    return jax.shard_map(
        on_device,
        mesh=mesh,
        in_specs=placed,
        out_specs=(P("row", None), P("row", "col")),
        check_vma=False,
    )
```
